256 devices in a mesh: group: 16 (over y_hi, x, core), seq: 16 (over z, y_lo).
Axes of the slice: x: 4, y: 4 (y_hi: 2, y_lo: 2; y = y_hi * 2 + y_lo), z: 8, core: 2. Of those that a mesh axis runs over, the one named last changes fastest.
Arguments:
- latent: float32 [32, 1024, 64], P('group', 'seq'), may hold values from -6 to 6
- margin_len: int32 [31], replicated, may hold values from 1 to 512, 11904 in all
- in_weight: bfloat16 [64, 1536], replicated, may hold values from -0.75 to 0.75
- norm_gain: float32 [1536], replicated, may hold values from 0.1 to 1.9
- qkv_weight: bfloat16 [3, 1536, 1024], P(None, None, 'seq'), may hold values from -0.15625 to 0.15625
- out_weight: bfloat16 [1024, 1536], P('seq'), may hold values from -0.1875 to 0.1875
- final_gain: float32 [1536], replicated, may hold values from 0.1 to 1.9
- head_out: bfloat16 [1536, 64], replicated, may hold values from -0.15625 to 0.15625
Outputs:
- next_latent: float32 [32, 1024, 64], P('group', 'seq')
The draws below stay inside these ranges and needn't reach their ends.
Inputs may be any that keep to these rules, and one draw needn't show every extreme that they name: `margin_len`: the lengths sum to 31 * (384) and the largest is exactly 512.
All inputs are finite; a program needn't handle non-finite values.
Results may differ from the reference program's by a relative error of at most 0.0024.
Values may be sent and summed in bfloat16 or wider, within the bound.
A program may use at most 128 MiB of HBM per device.

```python
import math
import jax
import jax.numpy as jnp
import numpy as np
from jax import lax

D = 1536
C = 64
HEADS = 16
HDIM = 64
CH = 1024
OVMAX = 512
NCH = 32
NOV = 31


def block_scale(rng, extent, cuts, least, largest):
    def one(axis_at, shards_of):
        heights = jax.random.uniform(jax.random.fold_in(jax.random.fold_in(rng, 6), axis_at), (shards_of,), jnp.float32, least / len(cuts), largest / len(cuts))
        return jnp.repeat(jnp.exp(heights), extent[axis_at] // shards_of).reshape((-1,) + (1,) * (len(extent) - axis_at - 1))

    level = one(*cuts[0])
    for cut in cuts[1:]:
        level = level * one(*cut)
    return level


def profile(count, total, limit, slope):
    loads = [(1 << 20) // math.isqrt(grade ** slope) + 1 for grade in range(2, count + 1)]
    spare, counts = total - limit - (count - 1), [1] * (count - 1)
    while spare > 0:
        candidates = [i for i in range(count - 1) if counts[i] < limit]
        pool, left = sum([loads[i] for i in candidates]), spare
        for i in candidates:
            addition = min(limit - counts[i], max(1, left * loads[i] // pool), spare)
            counts[i] = counts[i] + addition
            spare = spare - addition
    return np.array([limit] + counts)


def ragged_sizes(own_key, amount, total, limit, lean):
    if amount == 2:
        one = jax.random.randint(own_key, (), max(1, total - limit), min(limit, total - 1) + 1)
        return jnp.stack([one, total - one])
    tallies = jnp.asarray(profile(amount, total, limit, lean), jnp.int32)
    couples = (amount - 1) // 2
    donor, sink = tallies[1:1 + 2 * couples:2], tallies[2:2 + 2 * couples:2]
    margin = jnp.minimum(donor - 1, limit - sink)
    passed = jax.random.randint(jax.random.fold_in(own_key, 1), (couples,), 0, 1 << 20) % (margin + 1)
    tallies = tallies.at[1:1 + 2 * couples:2].set(donor - passed).at[2:2 + 2 * couples:2].set(sink + passed)
    return tallies[jax.random.permutation(jax.random.fold_in(own_key, 2), amount)]


def noise(rng, dims, scale, limit, cuts=(), kind=jnp.bfloat16):
    array = scale * jax.random.normal(rng, dims, jnp.float32)
    if cuts:
        array = array * block_scale(rng, dims, cuts, -0.22, 0.18)
    return jnp.clip(array, -limit, limit).astype(kind)


def setup_inputs(seed: int = 0) -> dict:
    keys = jax.random.split(jax.random.key(seed), 9)
    latent = noise(keys[0], (NCH, CH, C), 1.0, 6.0, ((0, 16), (1, 16)), jnp.float32)
    margin_len = ragged_sizes(keys[1], NOV, NOV * (3 * OVMAX // 4), OVMAX, 1).astype(jnp.int32)
    in_weight = noise(keys[2], (C, D), C ** -0.5, 0.75)
    norm_gain = jnp.clip(1.0 + 0.18 * jax.random.normal(keys[3], (D,), jnp.float32), 0.1, 1.9)
    qkv_weight = noise(keys[4], (3, D, HEADS * HDIM), D ** -0.5, 0.15625, ((2, 16),))
    out_weight = noise(keys[5], (HEADS * HDIM, D), (HEADS * HDIM) ** -0.5, 0.1875, ((0, 16),))
    final_gain = jnp.clip(1.0 + 0.18 * jax.random.normal(keys[6], (D,), jnp.float32), 0.1, 1.9)
    head_out = noise(keys[7], (D, C), D ** -0.5, 0.15625)
    return dict(latent=latent, margin_len=margin_len, in_weight=in_weight, norm_gain=norm_gain, qkv_weight=qkv_weight, out_weight=out_weight, final_gain=final_gain, head_out=head_out)


STEP = -0.5

def layer_norm(values_in, gain):
    row_mean = lax.optimization_barrier(jnp.mean(values_in, axis=-1, keepdims=True))
    centered = values_in - row_mean
    variance = lax.optimization_barrier(jnp.mean(centered * centered, axis=-1, keepdims=True))
    return centered / jnp.sqrt(variance + 1e-05) * gain.astype(jnp.float32)

def rms_heads(values_in):
    return values_in / jnp.sqrt(lax.optimization_barrier(jnp.mean(values_in * values_in, axis=-1, keepdims=True)) + 1e-06)

def node_block(window, key_count, in_weight, norm_gain, qkv_weight, out_weight, final_gain, head_out):
    tokens = window.shape[0]
    inputs = jnp.dot(window.astype(jnp.bfloat16), in_weight, preferred_element_type=jnp.float32)
    normed = layer_norm(inputs, norm_gain).astype(jnp.bfloat16)
    queries = jnp.dot(normed, qkv_weight[0], preferred_element_type=jnp.float32).reshape(tokens, HEADS, HDIM)
    keys_all = jnp.dot(normed, qkv_weight[1], preferred_element_type=jnp.float32).reshape(tokens, HEADS, HDIM)
    values = jnp.dot(normed, qkv_weight[2], preferred_element_type=jnp.float32).reshape(tokens, HEADS, HDIM)
    queries = rms_heads(queries).astype(jnp.bfloat16)
    keys_all = rms_heads(keys_all).astype(jnp.bfloat16)
    values = values.astype(jnp.bfloat16)
    scores = jnp.einsum('qhd,khd->hqk', queries.astype(jnp.float32), keys_all.astype(jnp.float32))
    key_mask = (jnp.arange(tokens) < key_count).astype(jnp.float32)
    exp_scores = jnp.exp(scores * HDIM ** (-0.5)) * key_mask[None, None, :]
    weights = (exp_scores / lax.optimization_barrier(jnp.sum(exp_scores, axis=-1, keepdims=True))).astype(jnp.bfloat16)
    attention = jnp.einsum('hqk,khd->qhd', weights.astype(jnp.float32), values.astype(jnp.float32))
    attention = attention.astype(jnp.bfloat16).reshape(tokens, HEADS * HDIM)
    mixed = inputs + jnp.dot(attention, out_weight, preferred_element_type=jnp.float32)
    final_norm = layer_norm(mixed, final_gain).astype(jnp.bfloat16)
    return jnp.dot(final_norm, head_out, preferred_element_type=jnp.float32)

def reference(latent, margin_len, in_weight, norm_gain, qkv_weight, out_weight, final_gain, head_out):
    flat_latent = latent.reshape(NCH * CH, C)
    padded_len = jnp.concatenate([margin_len.astype(jnp.int32), jnp.zeros((1,), jnp.int32)])
    own_len = (CH - padded_len).astype(jnp.int32)
    positions = jnp.arange(CH, dtype=jnp.int32)
    group_ids = jnp.arange(NCH, dtype=jnp.int32)
    group_rows = jnp.where(positions[None, :] < own_len[:, None], group_ids[:, None] * CH + positions[None, :], (group_ids[:, None] + 1) * CH + positions[None, :] - own_len[:, None]).astype(jnp.int32)
    over_ids = jnp.arange(NOV, dtype=jnp.int32)
    spots = jnp.arange(OVMAX, dtype=jnp.int32)
    over_rows = ((over_ids[:, None] + 1) * CH + spots[None, :]).astype(jnp.int32)

    def run_group(rows_here):
        return node_block(jnp.take(flat_latent, rows_here, axis=0), CH, in_weight, norm_gain, qkv_weight, out_weight, final_gain, head_out)

    def run_margin(pair):
        return node_block(jnp.take(flat_latent, pair[0], axis=0), pair[1], in_weight, norm_gain, qkv_weight, out_weight, final_gain, head_out)
    group_scores = lax.map(run_group, group_rows)
    over_scores = lax.map(run_margin, (over_rows, margin_len.astype(jnp.int32)))
    counted = (spots[None, :] < margin_len[:, None]).astype(jnp.float32)
    signed = -over_scores * counted[:, :, None]
    assembled = jnp.zeros((NCH * CH, C), jnp.float32)
    assembled = assembled.at[group_rows.reshape(-1)].add(group_scores.reshape(-1, C))
    assembled = assembled.at[over_rows.reshape(-1)].add(signed.reshape(-1, C))
    keep_rows = positions[None, :] < own_len[:, None]
    return jnp.where(keep_rows[:, :, None], latent + STEP * assembled.reshape(NCH, CH, C), jnp.float32(0.0))
```

```python
import functools
import math

import jax
import jax.numpy as jnp
from jax import lax
from jax.experimental import pallas as pl
from jax.experimental.pallas import tpu as pltpu
from jax.sharding import PartitionSpec as P

MESH = pl.DeviceIdType.MESH
BF = jnp.bfloat16
F32 = jnp.float32

HDIM = 64
STEP = -0.5
ROWS = 64
PACK = 32
QSCALE = HDIM**-0.5 * math.log2(math.e)


def dot(a, b):
    return jnp.dot(a, b, preferred_element_type=F32)


def dot_nt(a, b):
    return lax.dot_general(a, b, (((1,), (1,)), ((), ())), preferred_element_type=F32)


def hi_lo(x):
    hi = x.astype(BF)
    return hi, (x - hi.astype(F32)).astype(BF)


def packed(x):
    return jnp.concatenate([x[:PACK], x[PACK:]], axis=1)


def unpacked(x):
    return jnp.concatenate([x[:, :HDIM], x[:, HDIM:]], axis=0)


def reversal():
    r = lax.broadcasted_iota(jnp.int32, (ROWS, ROWS), 0)
    c = lax.broadcasted_iota(jnp.int32, (ROWS, ROWS), 1)
    return (r + c == ROWS - 1).astype(F32)


def kernel(
    groups,
    lat_ref,
    lens_ref,
    wi_ref,
    gain_ref,
    qkv_hbm,
    o_hbm,
    fgain_ref,
    ho_hbm,
    out_ref,
    qkv_v,
    o_v,
    ho_v,
    lat_send,
    lat_buf,
    fold_buf,
    mo_buf,
    xkt,
    w_head,
    w_tail,
    att,
    sc_send,
    sc_recv,
    load_sem,
    lat_ssem,
    lat_rsem,
    fold_ssem,
    fold_rsem,
    z_ssem,
    y_ssem,
    sib_ssem,
    mo_rsem,
    sc_ssem,
    sc_rsem,
):
    g = lax.axis_index("group")
    s = lax.axis_index("seq")
    z = s // 2
    y = s % 2
    core = g % 2
    prev_g = (g + groups - 1) % groups
    next_g = (g + 1) % groups
    sib_g = g + 1 - 2 * core
    y_g = (g + core * (groups // 2)) % groups
    y_s = 2 * z + 1 - y
    low = s < 8
    half = mo_buf.shape[2]

    loads = [
        pltpu.make_async_copy(qkv_hbm, qkv_v, load_sem.at[0]),
        pltpu.make_async_copy(o_hbm, o_v, load_sem.at[1]),
        pltpu.make_async_copy(ho_hbm, ho_v, load_sem.at[2]),
    ]
    for load in loads:
        load.start()

    barrier = pltpu.get_barrier_semaphore()

    def greet(gg, ss):
        pl.semaphore_signal(barrier, inc=1, device_id=(gg, ss), device_id_type=MESH)

    @pl.loop(1, 16)
    def _(k):
        greet(g, (s + k) % 16)

    @pl.when(low)
    def _():
        @pl.loop(0, 8)
        def _(k):
            greet(prev_g, 2 * k + 1)

    @pl.when(y == 1)
    def _():
        @pl.loop(0, 8)
        def _(k):
            greet(next_g, k)

    greet(sib_g, s)

    @pl.when(core == 1)
    def _():
        greet(y_g, y_s)

    flip = reversal().astype(BF)
    main_at = jnp.where(low, s, 31 - s)
    for a in range(2):
        rows = lat_ref[a].astype(BF)
        turned = jnp.where(low, rows.astype(F32), dot(flip, rows))
        lat_send[a] = packed(turned).astype(BF)

    n_greet = 16 + jnp.where(low, 8, 0) + jnp.where(y == 1, 8, 0) + core
    pl.semaphore_wait(barrier, n_greet)

    def lat_copy(which, a, k, gg, ss, at):
        return pltpu.make_async_remote_copy(
            src_ref=lat_send.at[a],
            dst_ref=lat_buf.at[at],
            send_sem=lat_ssem.at[which, k],
            recv_sem=lat_rsem.at[at],
            device_id=(gg, ss),
            device_id_type=MESH,
        )

    def lat_sends(act):
        @pl.loop(0, 8)
        def _(j):
            k = (z + j) % 8
            for a in range(2):

                @pl.when(jnp.logical_or(j != 0, y != a))
                def _():
                    act(lat_copy(a, a, j, g, 2 * k + a, main_at))

            @pl.when(low)
            def _():
                @pl.when(jnp.logical_or(j != 0, y != 0))
                def _():
                    act(lat_copy(2, 1, j, g, 2 * k, 8 + s))

                act(lat_copy(3, 0, j, prev_g, 2 * k + 1, 8 + s))

    lat_sends(lambda c: c.start())
    lat_buf[main_at] = lat_send[y]

    @pl.when(jnp.logical_and(low, y == 0))
    def _():
        lat_buf[8 + s] = lat_send[1]

    wi = wi_ref[...].astype(F32)
    centred = wi - jnp.mean(wi, axis=1, keepdims=True)
    wg_hi, wg_lo = hi_lo(centred * gain_ref[...])
    wg = jnp.concatenate([wg_hi, wg_lo], axis=0)
    loads[0].wait()
    wqkv = jnp.concatenate([qkv_v[0], qkv_v[1], qkv_v[2]], axis=1)
    fold2 = dot(wg, wqkv)
    fold = fold2[:64] + fold2[64:]
    qk = jnp.concatenate([fold[:, :64], fold[:, 64:128]], axis=0)
    fold_buf[pl.ds(pl.multiple_of(s * 64, 64), 64), :] = qk.T.astype(BF)

    def fold_copy(k, ss, block):
        rows = pl.ds(pl.multiple_of(block * 64, 64), 64)
        return pltpu.make_async_remote_copy(
            src_ref=fold_buf.at[rows],
            dst_ref=fold_buf.at[rows],
            send_sem=fold_ssem.at[k],
            recv_sem=fold_rsem.at[block],
            device_id=(g, ss),
            device_id_type=MESH,
        )

    @pl.loop(1, 16)
    def _(k):
        fold_copy(k, (s + k) % 16, s).start()

    mv_hi, mv_lo = hi_lo(fold[:, 128:])
    loads[1].wait()
    mo = dot(mv_hi, o_v[...]) + dot(mv_lo, o_v[...])

    def mo_rows(block):
        return pl.ds(pl.multiple_of(block * 64, 64), 64)

    mo_buf[0, mo_rows(s), :] = mo[:, :half].astype(BF)
    mo_buf[1, mo_rows(s), :] = mo[:, half:].astype(BF)

    def mo_copy(part, block, ssem, gg, ss):
        return pltpu.make_async_remote_copy(
            src_ref=mo_buf.at[part, mo_rows(block)],
            dst_ref=mo_buf.at[part, mo_rows(block)],
            send_sem=ssem,
            recv_sem=mo_rsem.at[part, block],
            device_id=(gg, ss),
            device_id_type=MESH,
        )

    ahead = 1 - 2 * core

    def far(t):
        return 2 * ((z - ahead * t + 8) % 8) + y

    def near(t):
        return 2 * ((z + ahead * t + 8) % 8) + y

    z_next = 2 * ((z + ahead + 8) % 8) + y
    z_back = 2 * ((z - ahead + 8) % 8) + y

    def other(block):
        return block + 1 - 2 * y

    def ring_far(t):
        return mo_copy(core, far(t), z_ssem.at[0, t], g, z_next)

    def ring_near(t):
        return mo_copy(core, near(t), z_ssem.at[1, t], g, z_back)

    def across(block):
        return mo_copy(core, block, y_ssem.at[block // 2], y_g, y_s)

    def to_sib(block):
        return mo_copy(core, block, sib_ssem.at[block], sib_g, s)

    ring_far(0).start()
    ring_near(0).start()
    across(s).start()

    c_hi, c_lo = hi_lo(centred)
    cc = jnp.concatenate([c_hi, c_lo], axis=0)
    gram4 = dot_nt(cc, cc)
    gram2 = gram4[:64] + gram4[64:]
    gram = (gram2[:, :64] + gram2[:, 64:]) * (1.0 / wi.shape[1])
    gram_hi, gram_lo = hi_lo(gram)
    gram_st = jnp.concatenate([gram_hi, gram_lo], axis=0)

    def variance(xt):
        gx = dot(gram_st, xt.astype(BF))
        return jnp.maximum(jnp.sum((gx[:64] + gx[64:]) * xt, axis=0, keepdims=True), 0.0)

    node = 2 * g + y
    tail_len = jnp.where(node < lens_ref.shape[0], lens_ref[jnp.minimum(node, lens_ref.shape[0] - 1)], 0)

    @pl.loop(0, 8)
    def _(k):
        @pl.when(k != s)
        def _():
            lat_copy(0, 0, 0, g, s, k).wait_recv()

        @pl.when(jnp.logical_or(k != s, y != 0))
        def _():
            lat_copy(0, 0, 0, g, s, 8 + k).wait_recv()

        @pl.when(15 - k != s)
        def _():
            lat_copy(0, 0, 0, g, s, 16 + k).wait_recv()

    line = lax.broadcasted_iota(jnp.int32, (256, 128), 0)
    lane = lax.broadcasted_iota(jnp.int32, (256, 128), 1)
    spot = 64 * (line // 32) + line % 32 + 32 * (lane // 64)
    head_lines = lat_buf[0:8].astype(F32).reshape(256, 128)
    tail_lines = jnp.where(
        spot < tail_len,
        lat_buf[8:16].astype(F32).reshape(256, 128),
        lat_buf[16:24].astype(F32).reshape(256, 128),
    )
    tokens = jnp.concatenate([unpacked(head_lines), unpacked(tail_lines)], axis=0)
    xt = tokens.T
    xkt[0:64, :] = jnp.zeros((64, 1024), BF)
    xkt[64:128, :] = xt.astype(BF)
    var = variance(xt)
    key_eps = 1e-6 * (var + 1e-5)
    scaled = xt * lax.rsqrt(var + 1e-5)
    extra = (lax.broadcasted_iota(jnp.int32, (64, 1024), 0) == 0).astype(F32)
    w = jnp.concatenate([scaled, extra], axis=0).T
    w_head[...] = w[:512].astype(BF)
    place = lax.broadcasted_iota(jnp.int32, (512, 128), 0)
    tail_spot = 64 * ((place % 256) // 32) + place % 32 + 32 * (place // 256)
    w_tail[:, :128] = w[512:].astype(BF)
    w_tail[:, 128:] = jnp.where(tail_spot < tail_len, w[512:], 0.0).astype(BF)

    q_line = lax.broadcasted_iota(jnp.int32, (32, 128), 0)
    q_lane = lax.broadcasted_iota(jnp.int32, (32, 128), 1)
    q_spot = 64 * z + q_line + 32 * (q_lane // 64)
    q_tail = jnp.where(q_spot < tail_len, lat_buf[8 + z].astype(F32), lat_buf[16 + z].astype(F32))
    q_tok = jnp.concatenate([unpacked(lat_buf[z].astype(F32)), unpacked(q_tail)], axis=0)
    q_xt = q_tok.T
    q_eps = 1e-6 * (variance(q_xt) + 1e-5)
    q_xtz = jnp.concatenate([q_xt.astype(BF), jnp.zeros((64, 128), BF)], axis=0)
    q_side = lax.broadcasted_iota(jnp.int32, (128, 128), 1) < 64

    def rms(x, eps, scale):
        parts = []
        for h in range(2):
            rows = x[64 * h : 64 * h + 64]
            mean = jnp.sum(rows * rows, axis=0, keepdims=True) * (1.0 / HDIM)
            parts.append(rows * (lax.rsqrt(mean + eps) * scale))
        return jnp.concatenate(parts, axis=0)

    @pl.loop(0, 8)
    def _(n):
        off = jnp.where(n % 2 == 1, (n + 1) // 2, 8 - n // 2)
        zz = (z + off) % 8
        for h in range(2):

            @pl.when(2 * zz + h != s)
            def _():
                fold_copy(0, s, 2 * zz + h).wait_recv()

        pair = fold_buf[pl.ds(pl.multiple_of(zz * 128, 128), 128), :]
        keys_t = rms(dot(pair, xkt[...]), key_eps, 1.0).astype(BF)
        query = rms(dot(pair, q_xtz), q_eps, QSCALE).T
        query2 = jnp.concatenate(
            [jnp.where(q_side, query, 0.0), jnp.where(q_side, 0.0, query)], axis=0
        ).astype(BF)
        p = jnp.exp2(dot(query2, keys_t)).astype(BF)
        u_head = dot(p[:, :512], w_head[...])
        u_tail = dot(p[:, 512:], w_tail[...])
        u_all = u_head + u_tail[:, :128]
        ratio = u_all[:, :64] / u_all[:, 64:65]
        u_over = jnp.concatenate([u_tail[64:128, 128:], u_tail[192:256, 128:]], axis=0)
        total = u_over[:, 64:65]
        over = u_over[:, :64] / jnp.where(total == 0.0, 1.0, total)
        columns = pl.ds(pl.multiple_of(zz * 128, 128), 128)
        att[0:128, columns] = jnp.concatenate([ratio[:128], ratio[128:]], axis=1).astype(BF)
        att[128:192, columns] = jnp.concatenate([over[:64], over[64:]], axis=1).astype(BF)

        t = (n + 1) // 2

        @pl.when(n % 2 == 1)
        def _():
            mo_copy(core, far(t), z_ssem.at[0, 0], g, s).wait_recv()

            @pl.when(t < 4)
            def _():
                ring_far(t).start()
                mo_copy(core, near(t), z_ssem.at[0, 0], g, s).wait_recv()

                @pl.when(t < 3)
                def _():
                    ring_near(t).start()

                across(near(t)).start()
                to_sib(near(t)).start()

            across(far(t)).start()
            to_sib(far(t)).start()

            mo_copy(core, other(far(t - 1)), z_ssem.at[0, 0], g, s).wait_recv()
            to_sib(other(far(t - 1))).start()

            @pl.when(t > 1)
            def _():
                mo_copy(core, other(near(t - 1)), z_ssem.at[0, 0], g, s).wait_recv()
                to_sib(other(near(t - 1))).start()

    last = other(far(4))
    mo_copy(core, last, z_ssem.at[0, 0], g, s).wait_recv()
    to_sib(last).start()

    @pl.loop(1, 16)
    def _(k):
        mo_copy(1 - core, (s + k) % 16, z_ssem.at[0, 0], g, s).wait_recv()

    tok2 = jnp.concatenate([q_tok, q_tok[64:]], axis=0).astype(BF)
    mixed = jnp.concatenate(
        [
            dot(att[...], mo_buf[k]) + dot(tok2, wi_ref[:, k * half : (k + 1) * half])
            for k in range(2)
        ],
        axis=1,
    )
    mean = jnp.mean(mixed, axis=1, keepdims=True)
    centre = mixed - mean
    spread = jnp.mean(centre * centre, axis=1, keepdims=True)
    loads[2].wait()
    final = (centre * lax.rsqrt(spread + 1e-5) * fgain_ref[...]).astype(BF)
    score = dot(final, ho_v[...])

    where_t = 64 * z + lax.broadcasted_iota(jnp.int32, (64, 64), 0)
    counted = where_t < tail_len
    sc_send[0] = score[:64]
    sc_send[1] = jnp.where(counted, score[64:128] - score[128:], 0.0)
    sc_send[2] = jnp.dot(
        reversal(),
        jnp.where(counted, 0.0, score[64:128]),
        precision=lax.Precision.HIGHEST,
        preferred_element_type=F32,
    )

    tail_g = jnp.where(y == 0, g, next_g)
    targets = [(g, z, y), (tail_g, z, 3 - y), (g, 15 - z, y)]

    def sc_copy(k, gg, ss, at):
        return pltpu.make_async_remote_copy(
            src_ref=sc_send.at[k],
            dst_ref=sc_recv.at[at],
            send_sem=sc_ssem.at[k],
            recv_sem=sc_rsem.at[at],
            device_id=(gg, ss),
            device_id_type=MESH,
        )

    def own(k):
        if k == 0:
            return s == z
        if k == 1:
            return jnp.logical_and(y == 0, s == z)
        return s == 15 - z

    for k, (gg, ss, at) in enumerate(targets):

        @pl.when(jnp.logical_not(own(k)))
        def _():
            sc_copy(k, gg, ss, at).start()

        @pl.when(own(k))
        def _():
            sc_recv[at] = sc_send[k]

    @pl.when(jnp.logical_not(low))
    def _():
        sc_recv[2] = jnp.zeros((64, 64), F32)
        sc_recv[3] = jnp.zeros((64, 64), F32)

    @pl.when(jnp.logical_and(s != 0, s != 10))
    def _():
        sc_copy(0, g, s, 0).wait_recv()

    sc_copy(0, g, s, 1).wait_recv()

    @pl.when(low)
    def _():
        sc_copy(0, g, s, 2).wait_recv()

        @pl.when(s != 0)
        def _():
            sc_copy(0, g, s, 3).wait_recv()

    row = 64 * s + lax.broadcasted_iota(jnp.int32, (64, 64), 0)
    for a in range(2):
        slot = 2 * g + a
        gone = jnp.where(slot < lens_ref.shape[0], lens_ref[jnp.minimum(slot, lens_ref.shape[0] - 1)], 0)
        step = lat_ref[a] + STEP * (sc_recv[a] + sc_recv[2 + a])
        out_ref[a] = jnp.where(row < 1024 - gone, step, 0.0)

    lat_sends(lambda c: c.wait_send())

    @pl.loop(1, 16)
    def _(k):
        fold_copy(k, s, s).wait_send()
        to_sib((s + k) % 16).wait_send()

    for t in range(4):
        ring_far(t).wait_send()
    for t in range(3):
        ring_near(t).wait_send()

    @pl.loop(0, 8)
    def _(k):
        across(2 * k + y).wait_send()

    for k in range(3):

        @pl.when(jnp.logical_not(own(k)))
        def _():
            sc_copy(k, g, s, 0).wait_send()


def solution(mesh):
    groups = mesh.shape["group"]

    def body(latent, margin_len, in_weight, norm_gain, qkv_weight, out_weight, final_gain, head_out):
        width = in_weight.shape[1]
        vmem = pl.BlockSpec(memory_space=pltpu.VMEM)
        hbm = pl.BlockSpec(memory_space=pl.ANY)
        dma = pltpu.SemaphoreType.DMA
        return pl.pallas_call(
            functools.partial(kernel, groups),
            out_shape=jax.ShapeDtypeStruct(latent.shape, F32),
            in_specs=[
                vmem,
                pl.BlockSpec(memory_space=pltpu.SMEM),
                vmem,
                vmem,
                hbm,
                hbm,
                vmem,
                hbm,
            ],
            out_specs=vmem,
            scratch_shapes=[
                pltpu.VMEM(qkv_weight.shape, BF),
                pltpu.VMEM(out_weight.shape, BF),
                pltpu.VMEM(head_out.shape, BF),
                pltpu.VMEM((2, PACK, 128), BF),
                pltpu.VMEM((24, PACK, 128), BF),
                pltpu.VMEM((1024, 128), BF),
                pltpu.VMEM((2, 1024, width // 2), BF),
                pltpu.VMEM((128, 1024), BF),
                pltpu.VMEM((512, 128), BF),
                pltpu.VMEM((512, 256), BF),
                pltpu.VMEM((192, 1024), BF),
                pltpu.VMEM((3, 64, 64), F32),
                pltpu.VMEM((4, 64, 64), F32),
                dma((3,)),
                dma((4, 8)),
                dma((24,)),
                dma((16,)),
                dma((16,)),
                dma((2, 4)),
                dma((8,)),
                dma((16,)),
                dma((2, 16)),
                dma((3,)),
                dma((4,)),
            ],
            compiler_params=pltpu.CompilerParams(
                collective_id=0, has_side_effects=True, vmem_limit_bytes=48 * 1024 * 1024
            ),
        )(
            latent,
            margin_len,
            in_weight,
            norm_gain.reshape(1, width),
            qkv_weight,
            out_weight,
            final_gain.reshape(1, width),
            head_out,
        )

    in_specs = (
        P("group", "seq", None),
        P(),
        P(),
        P(),
        P(None, None, "seq"),
        P("seq", None),
        P(),
        P(),
    )
    return jax.shard_map(
        body, mesh=mesh, in_specs=in_specs, out_specs=P("group", "seq", None), check_vma=False
    )
```

```python
import functools
import math

import jax
import jax.numpy as jnp
from jax import lax
from jax.experimental import pallas as pl
from jax.experimental.pallas import tpu as pltpu
from jax.sharding import PartitionSpec as P

MESH = pl.DeviceIdType.MESH
BF = jnp.bfloat16
F32 = jnp.float32

HDIM = 64
STEP = -0.5
ROWS = 64
PACK = 32
QSCALE = HDIM**-0.5 * math.log2(math.e)


def dot(a, b):
    return jnp.dot(a, b, preferred_element_type=F32)


def dot_nt(a, b):
    return lax.dot_general(a, b, (((1,), (1,)), ((), ())), preferred_element_type=F32)


def hi_lo(x):
    hi = x.astype(BF)
    return hi, (x - hi.astype(F32)).astype(BF)


def packed(x):
    return jnp.concatenate([x[:PACK], x[PACK:]], axis=1)


def unpacked(x):
    return jnp.concatenate([x[:, :HDIM], x[:, HDIM:]], axis=0)


def reversal():
    r = lax.broadcasted_iota(jnp.int32, (ROWS, ROWS), 0)
    c = lax.broadcasted_iota(jnp.int32, (ROWS, ROWS), 1)
    return (r + c == ROWS - 1).astype(F32)


def kernel(
    groups,
    lat_hbm,
    lens_hbm,
    wi_hbm,
    gain_hbm,
    qkv_hbm,
    o_hbm,
    fgain_hbm,
    ho_hbm,
    out_ref,
    lat_ref,
    lens_ref,
    wi_ref,
    gain_ref,
    qkv_v,
    fgain_ref,
    ho_v,
    lat_send,
    lat_ht,
    lat_r,
    fold_buf,
    o_buf,
    xkt,
    w_head,
    w_tail,
    att,
    sc_send,
    sc_recv,
    load_sem,
    own_sem,
    lat_ssem,
    lat_rsem,
    fold_ssem,
    fsib_ssem,
    fold_rsem,
    z_ssem,
    y_ssem,
    x_ssem,
    sib_ssem,
    o_rsem,
    sc_ssem,
    sc_rsem,
):
    g = lax.axis_index("group")
    s = lax.axis_index("seq")
    z = s // 2
    y = s % 2
    core = g % 2
    prev_g = (g + groups - 1) % groups
    next_g = (g + 1) % groups
    sib_g = g + 1 - 2 * core
    y_g = (g + core * (groups // 2)) % groups
    y_s = 2 * z + 1 - y
    x = (g // 2) % 4
    px = x % 2
    x_step = jnp.where(core == 0, 1 - 2 * px, 2 * px - 1)
    x_g = g + 2 * ((x + x_step + 4) % 4 - x)
    mine = 2 * px + core
    low = s < 8
    quarter = o_buf.shape[2]

    def block_rows(block):
        return pl.ds(pl.multiple_of(block * 64, 64), 64)

    load_lat, load_lens, load_wi, load_gain, load_qkv, load_fgain, load_ho = [
        pltpu.make_async_copy(src, dst, load_sem.at[k])
        for k, (src, dst) in enumerate(
            [
                (lat_hbm, lat_ref),
                (lens_hbm, lens_ref),
                (wi_hbm, wi_ref),
                (gain_hbm, gain_ref),
                (qkv_hbm, qkv_v),
                (fgain_hbm, fgain_ref),
                (ho_hbm, ho_v),
            ]
        )
    ]
    load_o = [
        pltpu.make_async_copy(
            o_hbm.at[:, pl.ds(k * quarter, quarter)], o_buf.at[k, block_rows(s)], own_sem.at[k]
        )
        for k in range(4)
    ]
    for load in [load_lat, load_wi, load_gain, load_qkv, *load_o, load_lens, load_fgain, load_ho]:
        load.start()

    barrier = pltpu.get_barrier_semaphore()

    def greet(gg, ss):
        pl.semaphore_signal(barrier, inc=1, device_id=(gg, ss), device_id_type=MESH)

    @pl.loop(1, 16)
    def _(k):
        greet(g, (s + k) % 16)

    @pl.when(low)
    def _():
        @pl.loop(0, 8)
        def _(k):
            greet(prev_g, 2 * k + 1)

    @pl.when(y == 1)
    def _():
        @pl.loop(0, 8)
        def _(k):
            greet(next_g, k)

    greet(sib_g, s)
    greet(x_g, s)

    @pl.when(core == 1)
    def _():
        greet(y_g, y_s)

    flip = reversal().astype(BF)
    load_lat.wait()
    for a in range(2):
        rows = lat_ref[a].astype(BF)
        turned = jnp.where(low, rows.astype(F32), dot(flip, rows))
        lat_send[a] = packed(turned).astype(BF)

    n_greet = 17 + jnp.where(low, 8, 0) + jnp.where(y == 1, 8, 0) + core
    pl.semaphore_wait(barrier, n_greet)

    def lat_copy(src, dst, ssem, rsem, gg, ss):
        return pltpu.make_async_remote_copy(
            src_ref=src,
            dst_ref=dst,
            send_sem=ssem,
            recv_sem=lat_rsem.at[rsem],
            device_id=(gg, ss),
            device_id_type=MESH,
        )

    def lat_sends(act):
        @pl.loop(0, 8)
        def _(j):
            k = (z + j + 4) % 8
            near = j == 4

            @pl.when(low)
            def _():
                @pl.when(jnp.logical_not(jnp.logical_and(near, y == 0)))
                def _():
                    act(lat_copy(lat_send, lat_ht.at[s], lat_ssem.at[0, k], s, g, 2 * k))

                @pl.when(jnp.logical_not(jnp.logical_and(near, y == 1)))
                def _():
                    act(
                        lat_copy(
                            lat_send.at[1], lat_ht.at[s, 0], lat_ssem.at[1, k], s, g, 2 * k + 1
                        )
                    )

                act(
                    lat_copy(
                        lat_send.at[0],
                        lat_ht.at[s, 1],
                        lat_ssem.at[2, k],
                        8 + s,
                        prev_g,
                        2 * k + 1,
                    )
                )

            @pl.when(jnp.logical_not(low))
            def _():
                for a in range(2):

                    @pl.when(jnp.logical_not(jnp.logical_and(near, y == a)))
                    def _():
                        act(
                            lat_copy(
                                lat_send.at[a],
                                lat_r.at[15 - s],
                                lat_ssem.at[a, k],
                                31 - s,
                                g,
                                2 * k + a,
                            )
                        )

    lat_sends(lambda c: c.start())

    @pl.when(jnp.logical_and(low, y == 0))
    def _():
        lat_ht[s] = lat_send[...]

    @pl.when(jnp.logical_and(low, y == 1))
    def _():
        lat_ht[s, 0] = lat_send[1]

    @pl.when(jnp.logical_not(low))
    def _():
        lat_r[15 - s] = lat_send[y]

    def o_copy(part, block, ssem, gg, ss):
        return pltpu.make_async_remote_copy(
            src_ref=o_buf.at[part, block_rows(block)],
            dst_ref=o_buf.at[part, block_rows(block)],
            send_sem=ssem,
            recv_sem=o_rsem.at[part, block],
            device_id=(gg, ss),
            device_id_type=MESH,
        )

    def along(d):
        return o_copy(mine, s, z_ssem.at[d], g, 2 * ((z + d) % 8) + y)

    def across(block):
        return o_copy(mine, block, y_ssem.at[block // 2], y_g, y_s)

    def to_x(block):
        return o_copy(mine, block, x_ssem.at[block], x_g, s)

    def to_sib(part, block):
        return o_copy(part, block, sib_ssem.at[part // 2, block], sib_g, s)

    def arrived(part, block):
        o_copy(part, block, z_ssem.at[0], sib_g, s).wait_recv()

    for load in load_o:
        load.wait()
    for d in (4, 3, 5, 2, 6, 1, 7):
        along(d).start()
    across(s).start()

    load_wi.wait()
    load_gain.wait()
    wi = wi_ref[...].astype(F32)
    centred = wi - jnp.mean(wi, axis=1, keepdims=True)
    wg_hi, wg_lo = hi_lo(centred * gain_ref[...].reshape(1, -1))
    wg = jnp.concatenate([wg_hi, wg_lo], axis=0)
    load_qkv.wait()
    fold2 = dot_nt(qkv_v[...].reshape(192, -1), wg)
    fold = fold2[:, :64] + fold2[:, 64:]
    fold_buf[s, 0:64] = jnp.concatenate([fold[:64], fold[64:128]], axis=1).astype(BF)
    fold_buf[s, 64:96] = packed(fold[128:].T).astype(BF)

    def fold_copy(part, block, ssem, gg, ss):
        rows = pl.ds(pl.multiple_of(part * 48, 16), 48)
        return pltpu.make_async_remote_copy(
            src_ref=fold_buf.at[block, rows],
            dst_ref=fold_buf.at[block, rows],
            send_sem=ssem,
            recv_sem=fold_rsem.at[part, block],
            device_id=(gg, ss),
            device_id_type=MESH,
        )

    def fold_out(k):
        return fold_copy(core, s, fold_ssem.at[k], g, (s + k) % 16)

    def fold_sib(block):
        return fold_copy(core, block, fsib_ssem.at[block], sib_g, s)

    def fold_arrived(part, block):
        fold_copy(part, block, fold_ssem.at[0], sib_g, s).wait_recv()

    @pl.loop(0, 15)
    def _(k):
        fold_out((k + 8) % 16 + (k + 8) // 16).start()

    c_hi, c_lo = hi_lo(centred)
    cc = jnp.concatenate([c_hi, c_lo], axis=0)
    gram4 = dot_nt(cc, cc)
    gram2 = gram4[:64] + gram4[64:]
    gram = (gram2[:, :64] + gram2[:, 64:]) * (1.0 / wi.shape[1])
    gram_hi, gram_lo = hi_lo(gram)
    gram_st = jnp.concatenate([gram_hi, gram_lo], axis=0)

    def variance(xt):
        gx = dot(gram_st, xt.astype(BF))
        return jnp.maximum(jnp.sum((gx[:64] + gx[64:]) * xt, axis=0, keepdims=True), 0.0)

    load_lens.wait()
    node = 2 * g + y
    tail_len = jnp.where(node < lens_ref.shape[0], lens_ref[jnp.minimum(node, lens_ref.shape[0] - 1)], 0)

    def lat_arrived(dst, rsem):
        lat_copy(dst, dst, lat_ssem.at[0, 0], rsem, sib_g, s).wait_recv()

    @pl.loop(0, 8)
    def _(k):
        @pl.when(jnp.logical_and(y == 0, k != s))
        def _():
            lat_arrived(lat_ht.at[k], k)

        @pl.when(y == 1)
        def _():
            @pl.when(k != s)
            def _():
                lat_arrived(lat_ht.at[k, 0], k)

            lat_arrived(lat_ht.at[k, 1], 8 + k)

        @pl.when(15 - k != s)
        def _():
            lat_arrived(lat_r.at[k], 16 + k)

    line = lax.broadcasted_iota(jnp.int32, (256, 128), 0)
    lane = lax.broadcasted_iota(jnp.int32, (256, 128), 1)
    spot = 64 * (line // 32) + line % 32 + 32 * (lane // 64)
    head_lines = lat_ht[:, 0].astype(F32).reshape(256, 128)
    tail_lines = jnp.where(
        spot < tail_len,
        lat_ht[:, 1].astype(F32).reshape(256, 128),
        lat_r[...].astype(F32).reshape(256, 128),
    )
    tokens = jnp.concatenate([unpacked(head_lines), unpacked(tail_lines)], axis=0)
    xt = tokens.T
    xkt[0:64, :] = jnp.zeros((64, 1024), BF)
    xkt[64:128, :] = xt.astype(BF)
    var = variance(xt)
    key_eps = 1e-6 * (var + 1e-5)
    scaled = xt * lax.rsqrt(var + 1e-5)
    extra = (lax.broadcasted_iota(jnp.int32, (64, 1024), 0) == 0).astype(F32)
    w = jnp.concatenate([scaled, extra], axis=0).T
    w_head[...] = w[:512].astype(BF)
    place = lax.broadcasted_iota(jnp.int32, (512, 128), 0)
    tail_spot = 64 * ((place % 256) // 32) + place % 32 + 32 * (place // 256)
    w_tail[:, :128] = w[512:].astype(BF)
    w_tail[:, 128:] = jnp.where(tail_spot < tail_len, w[512:], 0.0).astype(BF)

    q_line = lax.broadcasted_iota(jnp.int32, (32, 128), 0)
    q_lane = lax.broadcasted_iota(jnp.int32, (32, 128), 1)
    q_spot = 64 * z + q_line + 32 * (q_lane // 64)
    q_tail = jnp.where(q_spot < tail_len, lat_ht[z, 1].astype(F32), lat_r[z].astype(F32))
    q_tok = jnp.concatenate([unpacked(lat_ht[z, 0].astype(F32)), unpacked(q_tail)], axis=0)
    q_xt = q_tok.T
    q_eps = 1e-6 * (variance(q_xt) + 1e-5)
    q_xtz = jnp.concatenate([q_xt.astype(BF), jnp.zeros((64, 128), BF)], axis=0)
    q_side = lax.broadcasted_iota(jnp.int32, (128, 128), 1) < 64

    def rms(x, eps, scale):
        parts = []
        for h in range(2):
            rows = x[64 * h : 64 * h + 64]
            mean = jnp.sum(rows * rows, axis=0, keepdims=True) * (1.0 / HDIM)
            parts.append(rows * (lax.rsqrt(mean + eps) * scale))
        return jnp.concatenate(parts, axis=0)

    def place(n):
        return (z + jnp.where(n % 2 == 1, (n + 1) // 2, 8 - n // 2)) % 8

    def fold_relay(n):
        for h in range(2):
            block = 2 * place(n) + h

            @pl.when(block != s)
            def _():
                fold_arrived(core, block)
                fold_sib(block).start()

    def out_of(d):
        return [2 * ((z + d) % 8) + y, 2 * ((z + 8 - d) % 8) + y]

    def pass_on_z(d):
        for k, block in enumerate(out_of(d)):

            @pl.when(jnp.logical_or(d != 4, k == 0))
            def _():
                arrived(mine, block)
                across(block).start()
                to_x(block).start()
                to_sib(mine, block).start()

    def pass_on_y(d):
        for k, block in enumerate(out_of(d)):

            @pl.when(jnp.logical_or(jnp.logical_and(d != 4, d != 0), k == 0))
            def _():
                other = block + 1 - 2 * y
                arrived(mine, other)
                to_x(other).start()
                to_sib(mine, other).start()

    theirs = 2 * (1 - px) + core

    def pass_on_x(d, side):
        for k, block in enumerate(out_of(d)):

            @pl.when(jnp.logical_or(jnp.logical_and(d != 4, d != 0), k == 0))
            def _():
                there = block + (1 - 2 * y) * side
                arrived(theirs, there)
                to_sib(theirs, there).start()

    fold_relay(0)

    @pl.loop(0, 8)
    def _(n):
        @pl.when(n < 7)
        def _():
            fold_relay(n + 1)

        zz = place(n)
        for h in range(2):

            @pl.when(2 * zz + h != s)
            def _():
                fold_arrived(1 - core, 2 * zz + h)

        pair = fold_buf[pl.ds(2 * zz, 2)]
        pair_qk = jnp.concatenate([pair[0, :64], pair[1, :64]], axis=0)
        keys_t = rms(dot(pair_qk, xkt[...]), key_eps, 1.0).astype(BF)
        query = rms(dot(pair_qk, q_xtz), q_eps, QSCALE).T
        query2 = jnp.concatenate(
            [jnp.where(q_side, query, 0.0), jnp.where(q_side, 0.0, query)], axis=0
        ).astype(BF)
        p = jnp.exp2(dot(query2, keys_t)).astype(BF)
        u_head = dot(p[:, :512], w_head[...])
        u_tail = dot(p[:, 512:], w_tail[...])
        u_all = u_head + u_tail[:, :128]
        ratio = u_all[:, :64] / u_all[:, 64:65]
        u_over = jnp.concatenate([u_tail[64:128, 128:], u_tail[192:256, 128:]], axis=0)
        total = u_over[:, 64:65]
        over = u_over[:, :64] / jnp.where(total == 0.0, 1.0, total)
        mean_even = jnp.concatenate([ratio[:128], over[:64]], axis=0).astype(BF)
        mean_odd = jnp.concatenate([ratio[128:], over[64:]], axis=0).astype(BF)
        att_even = dot(mean_even, unpacked(pair[0, 64:96].astype(F32)).astype(BF))
        att_odd = dot(mean_odd, unpacked(pair[1, 64:96].astype(F32)).astype(BF))
        columns = pl.ds(pl.multiple_of(zz * 128, 128), 128)
        att[:, columns] = jnp.concatenate([att_even, att_odd], axis=1).astype(BF)

        @pl.when(n < 4)
        def _():
            pass_on_z(n + 1)

        @pl.when(jnp.logical_and(n >= 2, n < 7))
        def _():
            pass_on_y(n - 2)

        @pl.when(n >= 4)
        def _():
            pass_on_x(n - 3, 0)

    @pl.loop(0, 5)
    def _(d):
        pass_on_x(d, 1)

    @pl.loop(1, 16)
    def _(k):
        for half in range(2):
            arrived(2 * half + 1 - core, (s + k) % 16)

    tok2 = jnp.concatenate([q_tok, q_tok[64:]], axis=0).astype(BF)
    mixed = jnp.concatenate(
        [
            dot(att[...], o_buf[k]) + dot(tok2, wi_ref[:, k * quarter : (k + 1) * quarter])
            for k in range(4)
        ],
        axis=1,
    )
    mean = jnp.mean(mixed, axis=1, keepdims=True)
    centre = mixed - mean
    spread = jnp.mean(centre * centre, axis=1, keepdims=True)
    load_fgain.wait()
    load_ho.wait()
    final = (centre * lax.rsqrt(spread + 1e-5) * fgain_ref[...].reshape(1, -1)).astype(BF)
    score = dot_nt(final, ho_v[...])

    where_t = 64 * z + lax.broadcasted_iota(jnp.int32, (64, 64), 0)
    counted = where_t < tail_len
    sc_send[0] = score[:64]
    sc_send[1] = jnp.where(counted, score[64:128] - score[128:], 0.0)
    sc_send[2] = jnp.dot(
        reversal(),
        jnp.where(counted, 0.0, score[64:128]),
        precision=lax.Precision.HIGHEST,
        preferred_element_type=F32,
    )

    tail_g = jnp.where(y == 0, g, next_g)
    targets = [(g, z, y), (tail_g, z, 3 - y), (g, 15 - z, y)]

    def sc_copy(k, gg, ss, at):
        return pltpu.make_async_remote_copy(
            src_ref=sc_send.at[k],
            dst_ref=sc_recv.at[at],
            send_sem=sc_ssem.at[k],
            recv_sem=sc_rsem.at[at],
            device_id=(gg, ss),
            device_id_type=MESH,
        )

    def own(k):
        if k == 0:
            return s == z
        if k == 1:
            return jnp.logical_and(y == 0, s == z)
        return s == 15 - z

    for k, (gg, ss, at) in enumerate(targets):

        @pl.when(jnp.logical_not(own(k)))
        def _():
            sc_copy(k, gg, ss, at).start()

        @pl.when(own(k))
        def _():
            sc_recv[at] = sc_send[k]

    @pl.when(jnp.logical_not(low))
    def _():
        sc_recv[2] = jnp.zeros((64, 64), F32)
        sc_recv[3] = jnp.zeros((64, 64), F32)

    @pl.when(jnp.logical_and(s != 0, s != 10))
    def _():
        sc_copy(0, g, s, 0).wait_recv()

    sc_copy(0, g, s, 1).wait_recv()

    @pl.when(low)
    def _():
        sc_copy(0, g, s, 2).wait_recv()

        @pl.when(s != 0)
        def _():
            sc_copy(0, g, s, 3).wait_recv()

    row = 64 * s + lax.broadcasted_iota(jnp.int32, (64, 64), 0)
    for a in range(2):
        slot = 2 * g + a
        gone = jnp.where(slot < lens_ref.shape[0], lens_ref[jnp.minimum(slot, lens_ref.shape[0] - 1)], 0)
        step = lat_ref[a] + STEP * (sc_recv[a] + sc_recv[2 + a])
        out_ref[a] = jnp.where(row < 1024 - gone, step, 0.0)

    lat_sends(lambda c: c.wait_send())

    @pl.loop(1, 16)
    def _(k):
        there = (s + k) % 16
        fold_out(k).wait_send()
        fold_sib(there).wait_send()
        to_x(there).wait_send()
        to_sib(mine, there).wait_send()
        to_sib(theirs, there).wait_send()

    @pl.loop(1, 8)
    def _(d):
        along(d).wait_send()

    @pl.loop(0, 8)
    def _(k):
        across(2 * k + y).wait_send()

    for k in range(3):

        @pl.when(jnp.logical_not(own(k)))
        def _():
            sc_copy(k, g, s, 0).wait_send()


def solution(mesh):
    groups = mesh.shape["group"]

    def body(latent, margin_len, in_weight, norm_gain, qkv_weight, out_weight, final_gain, head_out):
        width = in_weight.shape[1]
        vmem = pl.BlockSpec(memory_space=pltpu.VMEM)
        hbm = pl.BlockSpec(memory_space=pl.ANY)
        dma = pltpu.SemaphoreType.DMA
        return pl.pallas_call(
            functools.partial(kernel, groups),
            out_shape=jax.ShapeDtypeStruct(latent.shape, F32),
            in_specs=[hbm] * 8,
            out_specs=vmem,
            scratch_shapes=[
                pltpu.VMEM(latent.shape, F32),
                pltpu.SMEM(margin_len.shape, jnp.int32),
                pltpu.VMEM(in_weight.shape, BF),
                pltpu.VMEM((width,), F32),
                pltpu.VMEM((3, HDIM, width), BF),
                pltpu.VMEM((width,), F32),
                pltpu.VMEM(head_out.shape[::-1], BF),
                pltpu.VMEM((2, PACK, 128), BF),
                pltpu.VMEM((8, 2, PACK, 128), BF),
                pltpu.VMEM((8, PACK, 128), BF),
                pltpu.VMEM((16, 96, 128), BF),
                pltpu.VMEM((4, 1024, width // 4), BF),
                pltpu.VMEM((128, 1024), BF),
                pltpu.VMEM((512, 128), BF),
                pltpu.VMEM((512, 256), BF),
                pltpu.VMEM((192, 1024), BF),
                pltpu.VMEM((3, 64, 64), F32),
                pltpu.VMEM((4, 64, 64), F32),
                dma((7,)),
                dma((4,)),
                dma((3, 8)),
                dma((24,)),
                dma((16,)),
                dma((16,)),
                dma((2, 16)),
                dma((8,)),
                dma((8,)),
                dma((16,)),
                dma((2, 16)),
                dma((4, 16)),
                dma((3,)),
                dma((4,)),
            ],
            compiler_params=pltpu.CompilerParams(
                collective_id=0, has_side_effects=True, vmem_limit_bytes=60 * 1024 * 1024
            ),
        )(
            latent,
            margin_len,
            in_weight,
            norm_gain,
            jnp.swapaxes(qkv_weight, 1, 2),
            out_weight,
            final_gain,
            head_out.T,
        )

    in_specs = (
        P("group", "seq", None),
        P(),
        P(),
        P(),
        P(None, None, "seq"),
        P("seq", None),
        P(),
        P(),
    )
    return jax.shard_map(
        body, mesh=mesh, in_specs=in_specs, out_specs=P("group", "seq", None), check_vma=False
    )
```

```python
import functools
import math

import jax
import jax.numpy as jnp
from jax import lax
from jax.experimental import pallas as pl
from jax.experimental.pallas import tpu as pltpu
from jax.sharding import PartitionSpec as P

MESH = pl.DeviceIdType.MESH
BF = jnp.bfloat16
F32 = jnp.float32

HDIM = 64
STEP = -0.5
ROWS = 64
PACK = 32
QSCALE = HDIM**-0.5 * math.log2(math.e)


def dot(a, b):
    return jnp.dot(a, b, preferred_element_type=F32)


def dot_nt(a, b):
    return lax.dot_general(a, b, (((1,), (1,)), ((), ())), preferred_element_type=F32)


def hi_lo(x):
    hi = x.astype(BF)
    return hi, (x - hi.astype(F32)).astype(BF)


def packed(x):
    return jnp.concatenate([x[:PACK], x[PACK:]], axis=1)


def unpacked(x):
    return jnp.concatenate([x[:, :HDIM], x[:, HDIM:]], axis=0)


def reversal():
    r = lax.broadcasted_iota(jnp.int32, (ROWS, ROWS), 0)
    c = lax.broadcasted_iota(jnp.int32, (ROWS, ROWS), 1)
    return (r + c == ROWS - 1).astype(F32)


def kernel(
    groups,
    lat_hbm,
    lens_hbm,
    wi_hbm,
    gain_hbm,
    qkv_hbm,
    o_hbm,
    fgain_hbm,
    ho_hbm,
    out_ref,
    lat_ref,
    lens_ref,
    wi_ref,
    gain_ref,
    qkv_v,
    fgain_ref,
    ho_v,
    lat_send,
    lat_ht,
    lat_r,
    fold_buf,
    o_buf,
    xkt,
    w_head,
    w_tail,
    att,
    sc_send,
    sc_recv,
    load_sem,
    own_sem,
    lat_ssem,
    lat_rsem,
    fold_ssem,
    fy_ssem,
    fsib_ssem,
    fold_rsem,
    z_ssem,
    y_ssem,
    x_ssem,
    sib_ssem,
    o_rsem,
    sc_ssem,
    sc_rsem,
):
    g = lax.axis_index("group")
    s = lax.axis_index("seq")
    z = s // 2
    y = s % 2
    core = g % 2
    prev_g = (g + groups - 1) % groups
    next_g = (g + 1) % groups
    sib_g = g + 1 - 2 * core
    y_g = (g + core * (groups // 2)) % groups
    y_s = 2 * z + 1 - y
    x = (g // 2) % 4
    px = x % 2
    x_step = jnp.where(core == 0, 1 - 2 * px, 2 * px - 1)
    x_g = g + 2 * ((x + x_step + 4) % 4 - x)
    mine = 2 * px + core
    me = 8 * y + z
    low = s < 8
    head_block = (z + 2) % 8
    tail_block = jnp.where(z < 4, 4 * (z // 2) + 2 * (1 - z % 2), (2 * z + 5) % 8)
    quarter = o_buf.shape[2]

    def block_rows(block):
        return pl.ds(pl.multiple_of(block * 64, 64), 64)

    load_lat, load_lens, load_wi, load_gain, load_qkv, load_fgain, load_ho = [
        pltpu.make_async_copy(src, dst, load_sem.at[k])
        for k, (src, dst) in enumerate(
            [
                (lat_hbm, lat_ref),
                (lens_hbm, lens_ref),
                (wi_hbm, wi_ref),
                (gain_hbm, gain_ref),
                (qkv_hbm, qkv_v),
                (fgain_hbm, fgain_ref),
                (ho_hbm, ho_v),
            ]
        )
    ]
    load_o = [
        pltpu.make_async_copy(
            o_hbm.at[:, pl.ds(k * quarter, quarter)], o_buf.at[k, block_rows(me)], own_sem.at[k]
        )
        for k in range(4)
    ]
    for load in [load_lat, load_wi, load_gain, load_qkv, *load_o, load_lens, load_fgain, load_ho]:
        load.start()

    barrier = pltpu.get_barrier_semaphore()

    def greet(gg, ss):
        pl.semaphore_signal(barrier, inc=1, device_id=(gg, ss), device_id_type=MESH)

    @pl.loop(1, 16)
    def _(k):
        greet(g, (s + k) % 16)

    @pl.when(low)
    def _():
        @pl.loop(0, 8)
        def _(k):
            greet(prev_g, 2 * k + 1)

    @pl.when(y == 1)
    def _():
        @pl.loop(0, 8)
        def _(k):
            greet(next_g, k)

    greet(sib_g, s)
    greet(x_g, s)

    @pl.when(core == 1)
    def _():
        greet(y_g, y_s)

    flip = reversal().astype(BF)
    load_lat.wait()
    for a in range(2):
        rows = lat_ref[a].astype(BF)
        turned = jnp.where(low, rows.astype(F32), dot(flip, rows))
        lat_send[a] = packed(turned).astype(BF)

    n_greet = 17 + jnp.where(low, 8, 0) + jnp.where(y == 1, 8, 0) + core
    pl.semaphore_wait(barrier, n_greet)

    def lat_copy(src, dst, ssem, rsem, gg, ss):
        return pltpu.make_async_remote_copy(
            src_ref=src,
            dst_ref=dst,
            send_sem=ssem,
            recv_sem=lat_rsem.at[rsem],
            device_id=(gg, ss),
            device_id_type=MESH,
        )

    def lat_sends(act):
        @pl.loop(0, 8)
        def _(j):
            k = (z + j + 4) % 8
            near = j == 4

            @pl.when(low)
            def _():
                @pl.when(jnp.logical_not(jnp.logical_and(near, y == 0)))
                def _():
                    act(lat_copy(lat_send, lat_ht.at[s], lat_ssem.at[0, k], s, g, 2 * k))

                @pl.when(jnp.logical_not(jnp.logical_and(near, y == 1)))
                def _():
                    act(
                        lat_copy(
                            lat_send.at[1], lat_ht.at[s, 0], lat_ssem.at[1, k], s, g, 2 * k + 1
                        )
                    )

                act(
                    lat_copy(
                        lat_send.at[0],
                        lat_ht.at[s, 1],
                        lat_ssem.at[2, k],
                        8 + s,
                        prev_g,
                        2 * k + 1,
                    )
                )

            @pl.when(jnp.logical_not(low))
            def _():
                for a in range(2):

                    @pl.when(jnp.logical_not(jnp.logical_and(near, y == a)))
                    def _():
                        act(
                            lat_copy(
                                lat_send.at[a],
                                lat_r.at[15 - s],
                                lat_ssem.at[a, k],
                                31 - s,
                                g,
                                2 * k + a,
                            )
                        )

    lat_sends(lambda c: c.start())

    @pl.when(jnp.logical_and(low, y == 0))
    def _():
        lat_ht[s] = lat_send[...]

    @pl.when(jnp.logical_and(low, y == 1))
    def _():
        lat_ht[s, 0] = lat_send[1]

    @pl.when(jnp.logical_not(low))
    def _():
        lat_r[15 - s] = lat_send[y]

    def o_copy(part, block, ssem, gg, ss):
        return pltpu.make_async_remote_copy(
            src_ref=o_buf.at[part, block_rows(block)],
            dst_ref=o_buf.at[part, block_rows(block)],
            send_sem=ssem,
            recv_sem=o_rsem.at[part, block],
            device_id=(gg, ss),
            device_id_type=MESH,
        )

    def seq_at(d):
        return 2 * ((z + d + 8) % 8) + y

    def column(d):
        return 8 * y + (z + d + 8) % 8

    def other(d):
        return 8 * (1 - y) + (z + d + 8) % 8

    def along(k, d):
        return o_copy(mine, me, z_ssem.at[k], g, seq_at(d))

    firsts = [along(k, d) for k, d in enumerate((2, -2, 1, -1))]
    side = 1 - 2 * core
    on_up = o_copy(mine, column(-2), z_ssem.at[4], g, seq_at(1))
    on_down = o_copy(mine, column(2), z_ssem.at[5], g, seq_at(-1))
    on_far = o_copy(mine, column(-2 * side), z_ssem.at[6], g, seq_at(2 * side))

    def across(block):
        return o_copy(mine, block, y_ssem.at[block % 8], y_g, y_s)

    def to_x(block):
        return o_copy(mine, block, x_ssem.at[block], x_g, s)

    def to_sib(part, block):
        return o_copy(part, block, sib_ssem.at[part // 2, block], sib_g, s)

    def arrived(part, block):
        o_copy(part, block, z_ssem.at[0], sib_g, s).wait_recv()

    load_wi.wait()
    load_gain.wait()
    wi = wi_ref[...].astype(F32)
    centred = wi - jnp.mean(wi, axis=1, keepdims=True)
    wg_hi, wg_lo = hi_lo(centred * gain_ref[...].reshape(1, -1))
    wg = jnp.concatenate([wg_hi, wg_lo], axis=0)
    load_qkv.wait()
    fold2 = dot_nt(qkv_v[...].reshape(192, -1), wg)
    fold = fold2[:, :64] + fold2[:, 64:]
    fold_buf[me, 0:64] = jnp.concatenate([fold[:64], fold[64:128]], axis=1).astype(BF)
    fold_buf[me, 64:96] = packed(fold[128:].T).astype(BF)

    def fold_copy(part, block, ssem, gg, ss):
        rows = pl.ds(pl.multiple_of(part * 48, 16), 48)
        return pltpu.make_async_remote_copy(
            src_ref=fold_buf.at[block, rows],
            dst_ref=fold_buf.at[block, rows],
            send_sem=ssem,
            recv_sem=fold_rsem.at[part, block],
            device_id=(gg, ss),
            device_id_type=MESH,
        )

    def fold_out(d):
        return fold_copy(core, me, fold_ssem.at[d], g, seq_at(d))

    def fold_across(block):
        return fold_copy(core, block, fy_ssem.at[block % 8], y_g, y_s)

    def fold_sib(block):
        return fold_copy(core, block, fsib_ssem.at[block], sib_g, s)

    def fold_arrived(part, block):
        fold_copy(part, block, fold_ssem.at[0], sib_g, s).wait_recv()

    fold_across(me).start()
    for d in (4, 3, 5, 2, 6, 1, 7):
        fold_out(d).start()

    for load in load_o:
        load.wait()
    for first in firsts:
        first.start()
    across(me).start()

    c_hi, c_lo = hi_lo(centred)
    cc = jnp.concatenate([c_hi, c_lo], axis=0)
    gram4 = dot_nt(cc, cc)
    gram2 = gram4[:64] + gram4[64:]
    gram = (gram2[:, :64] + gram2[:, 64:]) * (1.0 / wi.shape[1])
    gram_hi, gram_lo = hi_lo(gram)
    gram_st = jnp.concatenate([gram_hi, gram_lo], axis=0)

    def variance(xt):
        gx = dot(gram_st, xt.astype(BF))
        return jnp.maximum(jnp.sum((gx[:64] + gx[64:]) * xt, axis=0, keepdims=True), 0.0)

    load_lens.wait()
    node = 2 * g + y
    tail_len = jnp.where(node < lens_ref.shape[0], lens_ref[jnp.minimum(node, lens_ref.shape[0] - 1)], 0)

    def lat_arrived(dst, rsem):
        lat_copy(dst, dst, lat_ssem.at[0, 0], rsem, sib_g, s).wait_recv()

    @pl.loop(0, 8)
    def _(k):
        @pl.when(jnp.logical_and(y == 0, k != s))
        def _():
            lat_arrived(lat_ht.at[k], k)

        @pl.when(y == 1)
        def _():
            @pl.when(k != s)
            def _():
                lat_arrived(lat_ht.at[k, 0], k)

            lat_arrived(lat_ht.at[k, 1], 8 + k)

        @pl.when(15 - k != s)
        def _():
            lat_arrived(lat_r.at[k], 16 + k)

    line = lax.broadcasted_iota(jnp.int32, (256, 128), 0)
    lane = lax.broadcasted_iota(jnp.int32, (256, 128), 1)
    spot = 64 * (line // 32) + line % 32 + 32 * (lane // 64)
    head_lines = lat_ht[:, 0].astype(F32).reshape(256, 128)
    tail_lines = jnp.where(
        spot < tail_len,
        lat_ht[:, 1].astype(F32).reshape(256, 128),
        lat_r[...].astype(F32).reshape(256, 128),
    )
    tokens = jnp.concatenate([unpacked(head_lines), unpacked(tail_lines)], axis=0)
    xt = tokens.T
    xkt[0:64, :] = jnp.zeros((64, 1024), BF)
    xkt[64:128, :] = xt.astype(BF)
    var = variance(xt)
    key_eps = 1e-6 * (var + 1e-5)
    scaled = xt * lax.rsqrt(var + 1e-5)
    extra = (lax.broadcasted_iota(jnp.int32, (64, 1024), 0) == 0).astype(F32)
    w = jnp.concatenate([scaled, extra], axis=0).T
    w_head[...] = w[:512].astype(BF)
    place = lax.broadcasted_iota(jnp.int32, (512, 128), 0)
    tail_spot = 64 * ((place % 256) // 32) + place % 32 + 32 * (place // 256)
    w_tail[:, :128] = w[512:].astype(BF)
    w_tail[:, 128:] = jnp.where(tail_spot < tail_len, w[512:], 0.0).astype(BF)

    q_line = lax.broadcasted_iota(jnp.int32, (32, 128), 0)
    q_lane = lax.broadcasted_iota(jnp.int32, (32, 128), 1)
    q_spot = 64 * tail_block + q_line + 32 * (q_lane // 64)
    q_tail = jnp.where(q_spot < tail_len, lat_ht[tail_block, 1].astype(F32), lat_r[tail_block].astype(F32))
    q_tok = jnp.concatenate([unpacked(lat_ht[head_block, 0].astype(F32)), unpacked(q_tail)], axis=0)
    q_xt = q_tok.T
    q_eps = 1e-6 * (variance(q_xt) + 1e-5)
    q_xtz = jnp.concatenate([q_xt.astype(BF), jnp.zeros((64, 128), BF)], axis=0)
    q_side = lax.broadcasted_iota(jnp.int32, (128, 128), 1) < 64

    def rms(x, eps, scale):
        parts = []
        for h in range(2):
            rows = x[64 * h : 64 * h + 64]
            mean = jnp.sum(rows * rows, axis=0, keepdims=True) * (1.0 / HDIM)
            parts.append(rows * (lax.rsqrt(mean + eps) * scale))
        return jnp.concatenate(parts, axis=0)

    def at_step(n):
        turn = n % 4
        near = (z // 2 + jnp.where(turn < 2, turn, 5 - turn)) % 4
        return 8 * jnp.where(n < 4, y, 1 - y) + 2 * near

    def fold_relay(n):
        for h in range(2):
            block = at_step(n) + h

            @pl.when(block != me)
            def _():
                fold_arrived(core, block)

                @pl.when(n < 4)
                def _():
                    fold_across(block).start()

                fold_sib(block).start()

    def around(d, of):
        return [
            (of(d), d >= 0),
            (of(-d), jnp.logical_and(d != 0, d != 4)),
        ]

    def pass_on_z(i):
        d = jnp.where(i == 0, 2, jnp.where(i == 1, 1, i + 1))
        for block, there in around(d, column):

            @pl.when(there)
            def _():
                arrived(mine, block)
                across(block).start()
                to_x(block).start()
                to_sib(mine, block).start()

        @pl.when(i == 0)
        def _():
            on_up.start()
            on_down.start()
            on_far.start()

    def pass_on_y(i):
        d = jnp.where(i == 1, 2, jnp.where(i == 2, 1, i))
        for block, there in around(d, other):

            @pl.when(there)
            def _():
                arrived(mine, block)
                to_x(block).start()
                to_sib(mine, block).start()

    theirs = 2 * (1 - px) + core

    def pass_on_x(d, of):
        for block, there in around(d, of):

            @pl.when(there)
            def _():
                arrived(theirs, block)
                to_sib(theirs, block).start()

    fold_relay(0)
    fold_relay(1)

    @pl.loop(0, 8)
    def _(n):
        @pl.when(n < 6)
        def _():
            fold_relay(n + 2)

        first = at_step(n)
        for h in range(2):

            @pl.when(first + h != me)
            def _():
                fold_arrived(1 - core, first + h)

        pair = fold_buf[pl.ds(first, 2)]
        pair_qk = jnp.concatenate([pair[0, :64], pair[1, :64]], axis=0)
        keys_t = rms(dot(pair_qk, xkt[...]), key_eps, 1.0).astype(BF)
        query = rms(dot(pair_qk, q_xtz), q_eps, QSCALE).T
        query2 = jnp.concatenate(
            [jnp.where(q_side, query, 0.0), jnp.where(q_side, 0.0, query)], axis=0
        ).astype(BF)
        p = jnp.exp2(dot(query2, keys_t)).astype(BF)
        u_head = dot(p[:, :512], w_head[...])
        u_tail = dot(p[:, 512:], w_tail[...])
        u_all = u_head + u_tail[:, :128]
        ratio = u_all[:, :64] / u_all[:, 64:65]
        u_over = jnp.concatenate([u_tail[64:128, 128:], u_tail[192:256, 128:]], axis=0)
        total = u_over[:, 64:65]
        over = u_over[:, :64] / jnp.where(total == 0.0, 1.0, total)
        mean_even = jnp.concatenate([ratio[:128], over[:64]], axis=0).astype(BF)
        mean_odd = jnp.concatenate([ratio[128:], over[64:]], axis=0).astype(BF)
        att_even = dot(mean_even, unpacked(pair[0, 64:96].astype(F32)).astype(BF))
        att_odd = dot(mean_odd, unpacked(pair[1, 64:96].astype(F32)).astype(BF))
        columns = pl.ds(pl.multiple_of(first * 64, 128), 128)
        att[:, columns] = jnp.concatenate([att_even, att_odd], axis=1).astype(BF)

        @pl.when(n < 4)
        def _():
            pass_on_z(n)

        @pl.when(jnp.logical_and(n >= 1, n < 6))
        def _():
            pass_on_y(n - 1)

        @pl.when(jnp.logical_and(n >= 3, n < 7))
        def _():
            i = n - 3
            pass_on_x(jnp.where(i == 0, 2, jnp.where(i == 1, 1, i + 1)), column)

    for d in (0, 2, 1, 3, 4):
        pass_on_x(jnp.int32(d), other)

    @pl.loop(1, 16)
    def _(k):
        for half in range(2):
            arrived(2 * half + 1 - core, (me + k) % 16)

    tok2 = jnp.concatenate([q_tok, q_tok[64:]], axis=0).astype(BF)
    mixed = jnp.concatenate(
        [
            dot(att[...], o_buf[k]) + dot(tok2, wi_ref[:, k * quarter : (k + 1) * quarter])
            for k in range(4)
        ],
        axis=1,
    )
    mean = jnp.mean(mixed, axis=1, keepdims=True)
    centre = mixed - mean
    spread = jnp.mean(centre * centre, axis=1, keepdims=True)
    load_fgain.wait()
    load_ho.wait()
    final = (centre * lax.rsqrt(spread + 1e-5) * fgain_ref[...].reshape(1, -1)).astype(BF)
    score = dot_nt(final, ho_v[...])

    where_t = 64 * tail_block + lax.broadcasted_iota(jnp.int32, (64, 64), 0)
    counted = where_t < tail_len
    sc_send[0] = packed(score[:64])
    sc_send[1] = packed(jnp.where(counted, score[64:128] - score[128:], 0.0))
    turned = jnp.dot(
        reversal(),
        jnp.where(counted, 0.0, score[64:128]),
        precision=lax.Precision.HIGHEST,
        preferred_element_type=F32,
    )
    sc_send[2] = packed(turned)

    tail_g = jnp.where(y == 0, g, next_g)
    targets = [(g, head_block, y), (tail_g, tail_block, 3 - y), (g, 15 - tail_block, y)]

    def sc_copy(k, gg, ss, at):
        return pltpu.make_async_remote_copy(
            src_ref=sc_send.at[k],
            dst_ref=sc_recv.at[at],
            send_sem=sc_ssem.at[k],
            recv_sem=sc_rsem.at[at],
            device_id=(gg, ss),
            device_id_type=MESH,
        )

    own = [s == head_block, jnp.logical_and(y == 0, s == tail_block), s == 15 - tail_block]

    for k, (gg, ss, at) in enumerate(targets):

        @pl.when(jnp.logical_not(own[k]))
        def _():
            sc_copy(k, gg, ss, at).start()

        @pl.when(own[k])
        def _():
            sc_recv[at] = sc_send[k]

    @pl.when(jnp.logical_not(low))
    def _():
        sc_recv[2] = jnp.zeros((PACK, 128), F32)
        sc_recv[3] = jnp.zeros((PACK, 128), F32)

    kept = jnp.logical_or(own[0], own[2])
    for a in range(2):

        @pl.when(jnp.logical_not(jnp.logical_and(kept, y == a)))
        def _():
            sc_copy(0, g, s, a).wait_recv()

    @pl.when(low)
    def _():
        sc_copy(0, g, s, 2).wait_recv()

        @pl.when(jnp.logical_not(own[1]))
        def _():
            sc_copy(0, g, s, 3).wait_recv()

    row = 64 * s + lax.broadcasted_iota(jnp.int32, (64, 64), 0)
    for a in range(2):
        slot = 2 * g + a
        gone = jnp.where(slot < lens_ref.shape[0], lens_ref[jnp.minimum(slot, lens_ref.shape[0] - 1)], 0)
        step = lat_ref[a] + STEP * unpacked(sc_recv[a] + sc_recv[2 + a])
        out_ref[a] = jnp.where(row < 1024 - gone, step, 0.0)

    lat_sends(lambda c: c.wait_send())

    @pl.loop(1, 16)
    def _(k):
        there = (me + k) % 16
        fold_sib(there).wait_send()
        to_x(there).wait_send()
        to_sib(mine, there).wait_send()
        to_sib(theirs, there).wait_send()

    @pl.loop(1, 8)
    def _(d):
        fold_out(d).wait_send()

    for sent in (*firsts, on_up, on_down, on_far):
        sent.wait_send()

    @pl.loop(0, 8)
    def _(k):
        across(8 * y + k).wait_send()
        fold_across(8 * y + k).wait_send()

    for k in range(3):

        @pl.when(jnp.logical_not(own[k]))
        def _():
            sc_copy(k, g, s, 0).wait_send()


def solution(mesh):
    groups = mesh.shape["group"]

    def body(latent, margin_len, in_weight, norm_gain, qkv_weight, out_weight, final_gain, head_out):
        width = in_weight.shape[1]
        vmem = pl.BlockSpec(memory_space=pltpu.VMEM)
        hbm = pl.BlockSpec(memory_space=pl.ANY)
        dma = pltpu.SemaphoreType.DMA
        return pl.pallas_call(
            functools.partial(kernel, groups),
            out_shape=jax.ShapeDtypeStruct(latent.shape, F32),
            in_specs=[hbm] * 8,
            out_specs=vmem,
            scratch_shapes=[
                pltpu.VMEM(latent.shape, F32),
                pltpu.SMEM(margin_len.shape, jnp.int32),
                pltpu.VMEM(in_weight.shape, BF),
                pltpu.VMEM((width,), F32),
                pltpu.VMEM((3, HDIM, width), BF),
                pltpu.VMEM((width,), F32),
                pltpu.VMEM(head_out.shape[::-1], BF),
                pltpu.VMEM((2, PACK, 128), BF),
                pltpu.VMEM((8, 2, PACK, 128), BF),
                pltpu.VMEM((8, PACK, 128), BF),
                pltpu.VMEM((16, 96, 128), BF),
                pltpu.VMEM((4, 1024, width // 4), BF),
                pltpu.VMEM((128, 1024), BF),
                pltpu.VMEM((512, 128), BF),
                pltpu.VMEM((512, 256), BF),
                pltpu.VMEM((192, 1024), BF),
                pltpu.VMEM((3, PACK, 128), F32),
                pltpu.VMEM((4, PACK, 128), F32),
                dma((7,)),
                dma((4,)),
                dma((3, 8)),
                dma((24,)),
                dma((8,)),
                dma((8,)),
                dma((16,)),
                dma((2, 16)),
                dma((8,)),
                dma((8,)),
                dma((16,)),
                dma((2, 16)),
                dma((4, 16)),
                dma((3,)),
                dma((4,)),
            ],
            compiler_params=pltpu.CompilerParams(
                collective_id=0, has_side_effects=True, vmem_limit_bytes=60 * 1024 * 1024
            ),
        )(
            latent,
            margin_len,
            in_weight,
            norm_gain,
            jnp.swapaxes(qkv_weight, 1, 2),
            out_weight,
            final_gain,
            head_out.T,
        )

    in_specs = (
        P("group", "seq", None),
        P(),
        P(),
        P(),
        P(None, None, "seq"),
        P("seq", None),
        P(),
        P(),
    )
    return jax.shard_map(
        body, mesh=mesh, in_specs=in_specs, out_specs=P("group", "seq", None), check_vma=False
    )
```

```python
import functools
import math

import jax
import jax.numpy as jnp
from jax import lax
from jax.experimental import pallas as pl
from jax.experimental.pallas import tpu as pltpu
from jax.sharding import PartitionSpec as P

MESH = pl.DeviceIdType.MESH
BF = jnp.bfloat16
F32 = jnp.float32

HDIM = 64
STEP = -0.5
ROWS = 64
PACK = 32
QSCALE = HDIM**-0.5 * math.log2(math.e)


def dot(a, b):
    return jnp.dot(a, b, preferred_element_type=F32)


def dot_nt(a, b):
    return lax.dot_general(a, b, (((1,), (1,)), ((), ())), preferred_element_type=F32)


def hi_lo(x):
    hi = x.astype(BF)
    return hi, (x - hi.astype(F32)).astype(BF)


def packed(x):
    return jnp.concatenate([x[:PACK], x[PACK:]], axis=1)


def unpacked(x):
    return jnp.concatenate([x[:, :HDIM], x[:, HDIM:]], axis=0)


def reversal():
    r = lax.broadcasted_iota(jnp.int32, (ROWS, ROWS), 0)
    c = lax.broadcasted_iota(jnp.int32, (ROWS, ROWS), 1)
    return (r + c == ROWS - 1).astype(F32)


def kernel(
    groups,
    lat_hbm,
    lens_hbm,
    wi_hbm,
    gain_hbm,
    qkv_hbm,
    o_hbm,
    fgain_hbm,
    ho_hbm,
    out_ref,
    lat_ref,
    lens_ref,
    wi_ref,
    gain_ref,
    qkv_v,
    fgain_ref,
    ho_v,
    lat_send,
    lat_tok,
    lat_next,
    fold_buf,
    gram_buf,
    o_buf,
    xkt,
    w_head,
    w_tail,
    att,
    mix,
    sc_send,
    sc_recv,
    load_sem,
    own_sem,
    lat_ssem,
    lat_rsem,
    fold_ssem,
    fy_ssem,
    fsib_ssem,
    fold_rsem,
    z_ssem,
    y_ssem,
    x_ssem,
    sib_ssem,
    o_rsem,
    sc_ssem,
    sc_rsem,
):
    g = lax.axis_index("group")
    s = lax.axis_index("seq")
    z = s // 2
    y = s % 2
    core = g % 2
    prev_g = (g + groups - 1) % groups
    next_g = (g + 1) % groups
    sib_g = g + 1 - 2 * core
    y_g = (g + core * (groups // 2)) % groups
    y_s = 2 * z + 1 - y
    x = (g // 2) % 4
    px = x % 2
    x_step = jnp.where(core == 0, 1 - 2 * px, 2 * px - 1)
    x_g = g + 2 * ((x + x_step + 4) % 4 - x)
    mine = 2 * px + core
    me = 8 * y + z
    low = s < 8
    head_block = (z + 2) % 8
    tail_block = jnp.where(z < 4, 4 * (z // 2) + 2 * (1 - z % 2), (2 * z + 5) % 8)
    quarter = o_buf.shape[2]

    def block_rows(block):
        return pl.ds(pl.multiple_of(block * 64, 64), 64)

    load_lat, load_lens, load_wi, load_gain, load_qkv, load_fgain, load_ho = [
        pltpu.make_async_copy(src, dst, load_sem.at[k])
        for k, (src, dst) in enumerate(
            [
                (lat_hbm, lat_ref),
                (lens_hbm, lens_ref),
                (wi_hbm, wi_ref),
                (gain_hbm, gain_ref),
                (qkv_hbm, qkv_v),
                (fgain_hbm, fgain_ref),
                (ho_hbm, ho_v),
            ]
        )
    ]
    load_o = [
        pltpu.make_async_copy(
            o_hbm.at[:, pl.ds(k * quarter, quarter)], o_buf.at[k, block_rows(me)], own_sem.at[k]
        )
        for k in range(4)
    ]
    barrier = pltpu.get_barrier_semaphore()

    def greet(gg, ss):
        pl.semaphore_signal(barrier, inc=1, device_id=(gg, ss), device_id_type=MESH)

    @pl.loop(1, 16)
    def _(k):
        greet(g, (s + k) % 16)

    asker = jnp.where(
        s % 2 == 0, 2 * ((s % 8) // 4) + 1 - (s // 2) % 2, 4 + ((s + 3) % 8) // 2
    )
    greet(jnp.where(low, prev_g, next_g), 15 - s)

    @pl.when(low)
    def _():
        greet(prev_g, 2 * asker + 1)

    @pl.when(y == 1)
    def _():
        greet(next_g, tail_block)

    greet(sib_g, s)
    greet(x_g, s)

    @pl.when(core == 1)
    def _():
        greet(y_g, y_s)

    for load in [load_lat, load_wi, load_gain, load_qkv, *load_o, load_lens, load_fgain, load_ho]:
        load.start()

    flip = reversal().astype(BF)
    load_lat.wait()
    for a in range(2):
        rows = lat_ref[a].astype(BF)
        turned = jnp.where(low, rows.astype(F32), dot(flip, rows))
        lat_send[a] = packed(turned).astype(BF)

    def fold_weights():
        load_wi.wait()
        load_gain.wait()
        wi = wi_ref[...].astype(F32)
        centred = wi - jnp.mean(wi, axis=1, keepdims=True)
        wg_hi, wg_lo = hi_lo(centred * gain_ref[...].reshape(1, -1))
        wg = jnp.concatenate([wg_hi, wg_lo], axis=0)
        load_qkv.wait()
        fold2 = dot_nt(qkv_v[...].reshape(192, -1), wg)
        fold = fold2[:, :64] + fold2[:, 64:]
        fold_buf[me, 0:64] = jnp.concatenate([fold[:64], fold[64:128]], axis=1).astype(BF)
        fold_buf[me, 64:96] = packed(fold[128:].T).astype(BF)

        c_hi, c_lo = hi_lo(centred)
        cc = jnp.concatenate([c_hi, c_lo], axis=0)
        gram4 = dot_nt(cc, cc)
        gram2 = gram4[:64] + gram4[64:]
        gram_hi, gram_lo = hi_lo((gram2[:, :64] + gram2[:, 64:]) * (1.0 / wi.shape[1]))
        gram_buf[...] = jnp.concatenate([gram_hi, gram_lo], axis=0)

    fold_weights()

    n_greet = 18 + jnp.where(low, 1, 0) + y + core
    pl.semaphore_wait(barrier, n_greet)

    def lat_copy(src, dst, ssem, rsem, gg, ss):
        return pltpu.make_async_remote_copy(
            src_ref=src,
            dst_ref=dst,
            send_sem=ssem,
            recv_sem=lat_rsem.at[rsem],
            device_id=(gg, ss),
            device_id_type=MESH,
        )

    main_at = jnp.where(low, s, 23 - s)

    def lat_sends(act):
        @pl.loop(0, 8)
        def _(j):
            k = (z + j + 4) % 8
            for a in range(2):

                @pl.when(jnp.logical_not(jnp.logical_and(j == 4, y == a)))
                def _():
                    act(
                        lat_copy(
                            lat_send.at[a],
                            lat_tok.at[main_at],
                            lat_ssem.at[a, k],
                            main_at,
                            g,
                            2 * k + a,
                        )
                    )

    lat_early = [
        lat_copy(
            lat_send.at[1 - a],
            lat_next.at[a],
            lat_ssem.at[2, a],
            16 + a,
            g if a == 0 else prev_g,
            15 - s,
        )
        for a in range(2)
    ]

    @pl.when(low)
    def _():
        for early in lat_early:
            early.start()
        lat_sends(lambda c: c.start())

    def o_copy(part, block, ssem, gg, ss):
        return pltpu.make_async_remote_copy(
            src_ref=o_buf.at[part, block_rows(block)],
            dst_ref=o_buf.at[part, block_rows(block)],
            send_sem=ssem,
            recv_sem=o_rsem.at[part, block],
            device_id=(gg, ss),
            device_id_type=MESH,
        )

    def seq_at(d):
        return 2 * ((z + d + 8) % 8) + y

    def column(d):
        return 8 * y + (z + d + 8) % 8

    def other(d):
        return 8 * (1 - y) + (z + d + 8) % 8

    def along(k, d):
        return o_copy(mine, me, z_ssem.at[k], g, seq_at(d))

    firsts = [along(k, d) for k, d in enumerate((2, -2, 1, -1))]
    side = 1 - 2 * core
    on_up = o_copy(mine, column(-2), z_ssem.at[4], g, seq_at(1))
    on_down = o_copy(mine, column(2), z_ssem.at[5], g, seq_at(-1))
    on_far = o_copy(mine, column(-2 * side), z_ssem.at[6], g, seq_at(2 * side))

    def across(block):
        return o_copy(mine, block, y_ssem.at[block % 8], y_g, y_s)

    def to_x(block):
        return o_copy(mine, block, x_ssem.at[block], x_g, s)

    def to_sib(part, block):
        return o_copy(part, block, sib_ssem.at[part // 2, block], sib_g, s)

    def arrived(part, block):
        o_copy(part, block, z_ssem.at[0], sib_g, s).wait_recv()

    def fold_copy(part, block, ssem, gg, ss):
        rows = pl.ds(pl.multiple_of(part * 48, 16), 48)
        return pltpu.make_async_remote_copy(
            src_ref=fold_buf.at[block, rows],
            dst_ref=fold_buf.at[block, rows],
            send_sem=ssem,
            recv_sem=fold_rsem.at[part, block],
            device_id=(gg, ss),
            device_id_type=MESH,
        )

    def fold_out(d):
        return fold_copy(core, me, fold_ssem.at[d], g, seq_at(d))

    def fold_across(block):
        return fold_copy(core, block, fy_ssem.at[block % 8], y_g, y_s)

    def fold_sib(block):
        return fold_copy(core, block, fsib_ssem.at[block], sib_g, s)

    def fold_arrived(part, block):
        fold_copy(part, block, fold_ssem.at[0], sib_g, s).wait_recv()

    fold_across(me).start()
    for d in (4, 3, 5, 2, 6, 1, 7):
        fold_out(d).start()

    for load in load_o:
        load.wait()
    for first in firsts:
        first.start()
    across(me).start()

    load_lens.wait()

    def length(node):
        last = lens_ref.shape[0] - 1
        return jnp.where(node <= last, lens_ref[jnp.minimum(node, last)], 0)

    @pl.when(jnp.logical_not(low))
    def _():
        row = lax.broadcasted_iota(jnp.int32, (PACK, 128), 0)
        col = lax.broadcasted_iota(jnp.int32, (PACK, 128), 1)
        at = 64 * (15 - s) + row + 32 * (col // 64)
        for a in range(2):
            lat_early[a].wait_recv()
            lat_send[a] = jnp.where(
                at < length(2 * g + a), lat_next[a].astype(F32), lat_send[a].astype(F32)
            ).astype(BF)
        lat_sends(lambda c: c.start())

    lat_tok[main_at] = lat_send[y]

    def variance(xt):
        gx = dot(gram_buf[...], xt.astype(BF))
        return jnp.maximum(jnp.sum((gx[:64] + gx[64:]) * xt, axis=0, keepdims=True), 0.0)

    tail_len = length(2 * g + y)

    def at_step(n):
        turn = n % 4
        near = (z // 2 + jnp.where(turn < 2, turn, 5 - turn)) % 4
        return 8 * jnp.where(n < 4, y, 1 - y) + 2 * near

    def fold_relay(n):
        for h in range(2):
            block = at_step(n) + h

            @pl.when(block != me)
            def _():
                fold_arrived(core, block)

                @pl.when(n < 4)
                def _():
                    fold_across(block).start()

                fold_sib(block).start()

    def around(d, of):
        return [
            (of(d), d >= 0),
            (of(-d), jnp.logical_and(d != 0, d != 4)),
        ]

    def pass_on_z(i):
        d = jnp.where(i == 0, 2, jnp.where(i == 1, 1, i + 1))
        for block, there in around(d, column):

            @pl.when(there)
            def _():
                arrived(mine, block)
                across(block).start()
                to_x(block).start()
                to_sib(mine, block).start()

        @pl.when(i == 0)
        def _():
            on_up.start()
            on_down.start()
            on_far.start()

    def pass_on_y(i):
        d = jnp.where(i == 1, 2, jnp.where(i == 2, 1, i))
        for block, there in around(d, other):

            @pl.when(there)
            def _():
                arrived(mine, block)
                to_x(block).start()
                to_sib(mine, block).start()

    theirs = 2 * (1 - px) + core

    def pass_on_x(d, of):
        for block, there in around(d, of):

            @pl.when(there)
            def _():
                arrived(theirs, block)
                to_sib(theirs, block).start()

    for n in range(4):
        fold_relay(jnp.int32(n))

    @pl.loop(0, 16)
    def _(k):
        @pl.when(k != main_at)
        def _():
            lat_copy(lat_send.at[0], lat_tok.at[k], lat_ssem.at[0, 0], k, sib_g, s).wait_recv()

    head_lines = lat_tok[0:8].astype(F32).reshape(256, 128)
    tail_lines = lat_tok[8:16].astype(F32).reshape(256, 128)
    tokens = jnp.concatenate([unpacked(head_lines), unpacked(tail_lines)], axis=0)
    xt = tokens.T
    xkt[0:64, :] = jnp.zeros((64, 1024), BF)
    xkt[64:128, :] = xt.astype(BF)
    var = variance(xt)
    key_eps = 1e-6 * (var + 1e-5)
    scaled = xt * lax.rsqrt(var + 1e-5)
    extra = (lax.broadcasted_iota(jnp.int32, (64, 1024), 0) == 0).astype(F32)
    w = jnp.concatenate([scaled, extra], axis=0).T
    w_head[...] = w[:512].astype(BF)
    place = lax.broadcasted_iota(jnp.int32, (512, 128), 0)
    tail_spot = 64 * ((place % 256) // 32) + place % 32 + 32 * (place // 256)
    w_tail[:, :128] = w[512:].astype(BF)
    w_tail[:, 128:] = jnp.where(tail_spot < tail_len, w[512:], 0.0).astype(BF)

    q_tail = lat_tok[8 + tail_block].astype(F32)
    q_tok = jnp.concatenate([unpacked(lat_tok[head_block].astype(F32)), unpacked(q_tail)], axis=0)
    q_xt = q_tok.T
    q_eps = 1e-6 * (variance(q_xt) + 1e-5)
    q_xtz = jnp.concatenate([q_xt.astype(BF), jnp.zeros((64, 128), BF)], axis=0)
    q_side = lax.broadcasted_iota(jnp.int32, (128, 128), 1) < 64

    def rms(x, eps, scale):
        parts = []
        for h in range(2):
            rows = x[64 * h : 64 * h + 64]
            mean = jnp.sum(rows * rows, axis=0, keepdims=True) * (1.0 / HDIM)
            parts.append(rows * (lax.rsqrt(mean + eps) * scale))
        return jnp.concatenate(parts, axis=0)


    @pl.loop(0, 8)
    def _(n):
        @pl.when(n < 4)
        def _():
            fold_relay(n + 4)

        first = at_step(n)
        for h in range(2):

            @pl.when(first + h != me)
            def _():
                fold_arrived(1 - core, first + h)

        pair = fold_buf[pl.ds(first, 2)]
        pair_qk = jnp.concatenate([pair[0, :64], pair[1, :64]], axis=0)
        keys_t = rms(dot(pair_qk, xkt[...]), key_eps, 1.0).astype(BF)
        query = rms(dot(pair_qk, q_xtz), q_eps, QSCALE).T
        query2 = jnp.concatenate(
            [jnp.where(q_side, query, 0.0), jnp.where(q_side, 0.0, query)], axis=0
        ).astype(BF)
        p = jnp.exp2(dot(query2, keys_t)).astype(BF)
        u_head = dot(p[:, :512], w_head[...])
        u_tail = dot(p[:, 512:], w_tail[...])
        u_all = u_head + u_tail[:, :128]
        ratio = u_all[:, :64] / u_all[:, 64:65]
        u_over = jnp.concatenate([u_tail[64:128, 128:], u_tail[192:256, 128:]], axis=0)
        total = u_over[:, 64:65]
        over = u_over[:, :64] / jnp.where(total == 0.0, 1.0, total)
        mean_even = jnp.concatenate([ratio[:128], over[:64]], axis=0).astype(BF)
        mean_odd = jnp.concatenate([ratio[128:], over[64:]], axis=0).astype(BF)
        att_even = dot(mean_even, unpacked(pair[0, 64:96].astype(F32)).astype(BF))
        att_odd = dot(mean_odd, unpacked(pair[1, 64:96].astype(F32)).astype(BF))
        columns = pl.ds(pl.multiple_of(first * 64, 128), 128)
        att[:, columns] = jnp.concatenate([att_even, att_odd], axis=1).astype(BF)

        @pl.when(n < 4)
        def _():
            pass_on_z(n)

        @pl.when(jnp.logical_and(n >= 1, n < 6))
        def _():
            pass_on_y(n - 1)

        @pl.when(jnp.logical_and(n >= 3, n < 7))
        def _():
            i = n - 3
            pass_on_x(jnp.where(i == 0, 2, jnp.where(i == 1, 1, i + 1)), column)


    tok2 = jnp.concatenate([q_tok, q_tok[64:]], axis=0).astype(BF)
    def project(part):
        columns = pl.ds(pl.multiple_of(part * quarter, 128), quarter)
        mix[:, columns] = dot(att[...], o_buf[part]) + dot(tok2, wi_ref[:, columns])

    def from_sib(part):
        @pl.loop(1, 16)
        def _(k):
            arrived(part, (me + k) % 16)

    project(mine)
    from_sib(2 * px + 1 - core)
    project(2 * px + 1 - core)
    for d in (0, 2, 1, 3, 4):
        pass_on_x(jnp.int32(d), other)
    project(theirs)
    from_sib(2 * (1 - px) + 1 - core)
    project(2 * (1 - px) + 1 - core)
    mixed = mix[...]
    mean = jnp.mean(mixed, axis=1, keepdims=True)
    centre = mixed - mean
    spread = jnp.mean(centre * centre, axis=1, keepdims=True)
    load_fgain.wait()
    load_ho.wait()
    final = (centre * lax.rsqrt(spread + 1e-5) * fgain_ref[...].reshape(1, -1)).astype(BF)
    score = dot_nt(final, ho_v[...])

    where_t = 64 * tail_block + lax.broadcasted_iota(jnp.int32, (64, 64), 0)
    counted = where_t < tail_len
    sc_send[0] = packed(score[:64])
    sc_send[1] = packed(jnp.where(counted, score[64:128] - score[128:], 0.0))
    turned = jnp.dot(
        reversal(),
        jnp.where(counted, 0.0, score[64:128]),
        precision=lax.Precision.HIGHEST,
        preferred_element_type=F32,
    )
    sc_send[2] = packed(turned)

    tail_g = jnp.where(y == 0, g, next_g)
    targets = [(g, head_block, y), (tail_g, tail_block, 3 - y), (g, 15 - tail_block, y)]

    def sc_copy(k, gg, ss, at):
        return pltpu.make_async_remote_copy(
            src_ref=sc_send.at[k],
            dst_ref=sc_recv.at[at],
            send_sem=sc_ssem.at[k],
            recv_sem=sc_rsem.at[at],
            device_id=(gg, ss),
            device_id_type=MESH,
        )

    own = [s == head_block, jnp.logical_and(y == 0, s == tail_block), s == 15 - tail_block]

    for k, (gg, ss, at) in enumerate(targets):

        @pl.when(jnp.logical_not(own[k]))
        def _():
            sc_copy(k, gg, ss, at).start()

        @pl.when(own[k])
        def _():
            sc_recv[at] = sc_send[k]

    lat_sends(lambda c: c.wait_send())

    @pl.when(low)
    def _():
        for early in lat_early:
            early.wait_send()

    @pl.loop(1, 16)
    def _(k):
        there = (me + k) % 16
        fold_sib(there).wait_send()
        to_x(there).wait_send()
        to_sib(mine, there).wait_send()
        to_sib(theirs, there).wait_send()

    @pl.loop(1, 8)
    def _(d):
        fold_out(d).wait_send()

    for sent in (*firsts, on_up, on_down, on_far):
        sent.wait_send()

    @pl.loop(0, 8)
    def _(k):
        across(8 * y + k).wait_send()
        fold_across(8 * y + k).wait_send()

    @pl.when(jnp.logical_not(low))
    def _():
        sc_recv[2] = jnp.zeros((PACK, 128), F32)
        sc_recv[3] = jnp.zeros((PACK, 128), F32)

    kept = jnp.logical_or(own[0], own[2])
    for a in range(2):

        @pl.when(jnp.logical_not(jnp.logical_and(kept, y == a)))
        def _():
            sc_copy(0, g, s, a).wait_recv()

    @pl.when(low)
    def _():
        sc_copy(0, g, s, 2).wait_recv()

        @pl.when(jnp.logical_not(own[1]))
        def _():
            sc_copy(0, g, s, 3).wait_recv()

    row = 64 * s + lax.broadcasted_iota(jnp.int32, (64, 64), 0)
    for a in range(2):
        slot = 2 * g + a
        gone = length(slot)
        step = lat_ref[a] + STEP * unpacked(sc_recv[a] + sc_recv[2 + a])
        out_ref[a] = jnp.where(row < 1024 - gone, step, 0.0)

    for k in range(3):

        @pl.when(jnp.logical_not(own[k]))
        def _():
            sc_copy(k, g, s, 0).wait_send()


def solution(mesh):
    groups = mesh.shape["group"]

    def body(latent, margin_len, in_weight, norm_gain, qkv_weight, out_weight, final_gain, head_out):
        width = in_weight.shape[1]
        vmem = pl.BlockSpec(memory_space=pltpu.VMEM)
        hbm = pl.BlockSpec(memory_space=pl.ANY)
        dma = pltpu.SemaphoreType.DMA
        return pl.pallas_call(
            functools.partial(kernel, groups),
            out_shape=jax.ShapeDtypeStruct(latent.shape, F32),
            in_specs=[hbm] * 8,
            out_specs=vmem,
            scratch_shapes=[
                pltpu.VMEM(latent.shape, F32),
                pltpu.SMEM(margin_len.shape, jnp.int32),
                pltpu.VMEM(in_weight.shape, BF),
                pltpu.VMEM((width,), F32),
                pltpu.VMEM((3, HDIM, width), BF),
                pltpu.VMEM((width,), F32),
                pltpu.VMEM(head_out.shape[::-1], BF),
                pltpu.VMEM((2, PACK, 128), BF),
                pltpu.VMEM((16, PACK, 128), BF),
                pltpu.VMEM((2, PACK, 128), BF),
                pltpu.VMEM((16, 96, 128), BF),
                pltpu.VMEM((128, HDIM), BF),
                pltpu.VMEM((4, 1024, width // 4), BF),
                pltpu.VMEM((128, 1024), BF),
                pltpu.VMEM((512, 128), BF),
                pltpu.VMEM((512, 256), BF),
                pltpu.VMEM((192, 1024), BF),
                pltpu.VMEM((192, width), F32),
                pltpu.VMEM((3, PACK, 128), F32),
                pltpu.VMEM((4, PACK, 128), F32),
                dma((7,)),
                dma((4,)),
                dma((3, 8)),
                dma((24,)),
                dma((8,)),
                dma((8,)),
                dma((16,)),
                dma((2, 16)),
                dma((8,)),
                dma((8,)),
                dma((16,)),
                dma((2, 16)),
                dma((4, 16)),
                dma((3,)),
                dma((4,)),
            ],
            compiler_params=pltpu.CompilerParams(
                collective_id=0, has_side_effects=True, vmem_limit_bytes=60 * 1024 * 1024
            ),
        )(
            latent,
            margin_len,
            in_weight,
            norm_gain,
            jnp.swapaxes(qkv_weight, 1, 2),
            out_weight,
            final_gain,
            head_out.T,
        )

    in_specs = (
        P("group", "seq", None),
        P(),
        P(),
        P(),
        P(None, None, "seq"),
        P("seq", None),
        P(),
        P(),
    )
    return jax.shard_map(
        body, mesh=mesh, in_specs=in_specs, out_specs=P("group", "seq", None), check_vma=False
    )
```

```python
import functools
import math

import jax
import jax.numpy as jnp
from jax import lax
from jax.experimental import pallas as pl
from jax.experimental.pallas import tpu as pltpu
from jax.sharding import PartitionSpec as P

MESH = pl.DeviceIdType.MESH
BF = jnp.bfloat16
F32 = jnp.float32

HDIM = 64
STEP = -0.5
ROWS = 64
PACK = 32
QSCALE = HDIM**-0.5 * math.log2(math.e)


def dot(a, b):
    return jnp.dot(a, b, preferred_element_type=F32)


def dot_nt(a, b):
    return lax.dot_general(a, b, (((1,), (1,)), ((), ())), preferred_element_type=F32)


def hi_lo(x):
    hi = x.astype(BF)
    return hi, (x - hi.astype(F32)).astype(BF)


def packed(x):
    return jnp.concatenate([x[:PACK], x[PACK:]], axis=1)


def unpacked(x):
    return jnp.concatenate([x[:, :HDIM], x[:, HDIM:]], axis=0)


def reversal():
    r = lax.broadcasted_iota(jnp.int32, (ROWS, ROWS), 0)
    c = lax.broadcasted_iota(jnp.int32, (ROWS, ROWS), 1)
    return (r + c == ROWS - 1).astype(F32)


def kernel(
    groups,
    lat_hbm,
    lens_hbm,
    wi_hbm,
    gain_hbm,
    qkv_hbm,
    o_hbm,
    fgain_hbm,
    ho_hbm,
    out_ref,
    lat_ref,
    lens_ref,
    wi_ref,
    gain_ref,
    qkv_v,
    fgain_ref,
    ho_v,
    lat_send,
    lat_tok,
    lat_next,
    fold_buf,
    gram_buf,
    o_buf,
    xkt,
    w_head,
    w_tail,
    att,
    mix,
    key_buf,
    query_buf,
    sc_send,
    sc_recv,
    load_sem,
    own_sem,
    lat_ssem,
    lat_rsem,
    fold_ssem,
    fy_ssem,
    fsib_ssem,
    fold_rsem,
    z_ssem,
    y_ssem,
    x_ssem,
    sib_ssem,
    o_rsem,
    sc_ssem,
    sc_rsem,
):
    g = lax.axis_index("group")
    s = lax.axis_index("seq")
    z = s // 2
    y = s % 2
    core = g % 2
    prev_g = (g + groups - 1) % groups
    next_g = (g + 1) % groups
    sib_g = g + 1 - 2 * core
    y_g = (g + core * (groups // 2)) % groups
    y_s = 2 * z + 1 - y
    x = (g // 2) % 4
    px = x % 2
    x_step = jnp.where(core == 0, 1 - 2 * px, 2 * px - 1)
    x_g = g + 2 * ((x + x_step + 4) % 4 - x)
    mine = 2 * px + core
    me = 8 * y + z
    low = s < 8
    head_block = (z + 2) % 8
    tail_block = jnp.where(z < 4, 4 * (z // 2) + 2 * (1 - z % 2), (2 * z + 5) % 8)
    quarter = o_buf.shape[2]

    def block_rows(block):
        return pl.ds(pl.multiple_of(block * 64, 64), 64)

    load_lat, load_lens, load_wi, load_gain, load_qkv, load_fgain, load_ho = [
        pltpu.make_async_copy(src, dst, load_sem.at[k])
        for k, (src, dst) in enumerate(
            [
                (lat_hbm, lat_ref),
                (lens_hbm, lens_ref),
                (wi_hbm, wi_ref),
                (gain_hbm, gain_ref),
                (qkv_hbm, qkv_v),
                (fgain_hbm, fgain_ref),
                (ho_hbm, ho_v),
            ]
        )
    ]
    load_o = [
        pltpu.make_async_copy(
            o_hbm.at[:, pl.ds(k * quarter, quarter)], o_buf.at[k, block_rows(me)], own_sem.at[k]
        )
        for k in range(4)
    ]
    barrier = pltpu.get_barrier_semaphore()

    def greet(gg, ss):
        pl.semaphore_signal(barrier, inc=1, device_id=(gg, ss), device_id_type=MESH)

    @pl.loop(1, 16)
    def _(k):
        greet(g, (s + k) % 16)

    asker = jnp.where(
        s % 2 == 0, 2 * ((s % 8) // 4) + 1 - (s // 2) % 2, 4 + ((s + 3) % 8) // 2
    )
    greet(jnp.where(low, prev_g, next_g), 15 - s)

    @pl.when(low)
    def _():
        greet(prev_g, 2 * asker + 1)

    @pl.when(y == 1)
    def _():
        greet(next_g, tail_block)

    greet(sib_g, s)
    greet(x_g, s)

    @pl.when(core == 1)
    def _():
        greet(y_g, y_s)

    for load in [load_lat, load_wi, load_gain, load_qkv, *load_o, load_lens, load_fgain, load_ho]:
        load.start()

    flip = reversal().astype(BF)
    load_lat.wait()
    for a in range(2):
        rows = lat_ref[a].astype(BF)
        turned = jnp.where(low, rows.astype(F32), dot(flip, rows))
        lat_send[a] = packed(turned).astype(BF)

    def fold_weights():
        load_wi.wait()
        load_gain.wait()
        wi = wi_ref[...].astype(F32)
        centred = wi - jnp.mean(wi, axis=1, keepdims=True)
        wg_hi, wg_lo = hi_lo(centred * gain_ref[...].reshape(1, -1))
        wg = jnp.concatenate([wg_hi, wg_lo], axis=0)
        load_qkv.wait()
        fold2 = dot_nt(qkv_v[...].reshape(192, -1), wg)
        fold = fold2[:, :64] + fold2[:, 64:]
        fold_buf[me, 0:64] = jnp.concatenate([fold[:64], fold[64:128]], axis=1).astype(BF)
        fold_buf[me, 64:96] = packed(fold[128:].T).astype(BF)

        c_hi, c_lo = hi_lo(centred)
        cc = jnp.concatenate([c_hi, c_lo], axis=0)
        gram4 = dot_nt(cc, cc)
        gram2 = gram4[:64] + gram4[64:]
        gram_hi, gram_lo = hi_lo((gram2[:, :64] + gram2[:, 64:]) * (1.0 / wi.shape[1]))
        gram_buf[...] = jnp.concatenate([gram_hi, gram_lo], axis=0)

    fold_weights()

    n_greet = 18 + jnp.where(low, 1, 0) + y + core
    pl.semaphore_wait(barrier, n_greet)

    def lat_copy(src, dst, ssem, rsem, gg, ss):
        return pltpu.make_async_remote_copy(
            src_ref=src,
            dst_ref=dst,
            send_sem=ssem,
            recv_sem=lat_rsem.at[rsem],
            device_id=(gg, ss),
            device_id_type=MESH,
        )

    main_at = jnp.where(low, s, 23 - s)

    def lat_sends(act):
        @pl.loop(0, 8)
        def _(j):
            k = (z + j + 4) % 8
            for a in range(2):

                @pl.when(jnp.logical_not(jnp.logical_and(j == 4, y == a)))
                def _():
                    act(
                        lat_copy(
                            lat_send.at[a],
                            lat_tok.at[main_at],
                            lat_ssem.at[a, k],
                            main_at,
                            g,
                            2 * k + a,
                        )
                    )

    lat_early = [
        lat_copy(
            lat_send.at[1 - a],
            lat_next.at[a],
            lat_ssem.at[2, a],
            16 + a,
            g if a == 0 else prev_g,
            15 - s,
        )
        for a in range(2)
    ]

    @pl.when(low)
    def _():
        for early in lat_early:
            early.start()
        lat_sends(lambda c: c.start())

    def o_copy(part, block, ssem, gg, ss):
        return pltpu.make_async_remote_copy(
            src_ref=o_buf.at[part, block_rows(block)],
            dst_ref=o_buf.at[part, block_rows(block)],
            send_sem=ssem,
            recv_sem=o_rsem.at[part, block],
            device_id=(gg, ss),
            device_id_type=MESH,
        )

    def seq_at(d):
        return 2 * ((z + d + 8) % 8) + y

    def column(d):
        return 8 * y + (z + d + 8) % 8

    def other(d):
        return 8 * (1 - y) + (z + d + 8) % 8

    def along(k, d):
        return o_copy(mine, me, z_ssem.at[k], g, seq_at(d))

    firsts = [along(k, d) for k, d in enumerate((2, -2, 1, -1))]
    side = 1 - 2 * core
    on_up = o_copy(mine, column(-2), z_ssem.at[4], g, seq_at(1))
    on_down = o_copy(mine, column(2), z_ssem.at[5], g, seq_at(-1))
    on_far = o_copy(mine, column(-2 * side), z_ssem.at[6], g, seq_at(2 * side))

    def across(block):
        return o_copy(mine, block, y_ssem.at[block % 8], y_g, y_s)

    def to_x(block):
        return o_copy(mine, block, x_ssem.at[block], x_g, s)

    def to_sib(part, block):
        return o_copy(part, block, sib_ssem.at[part // 2, block], sib_g, s)

    def arrived(part, block):
        o_copy(part, block, z_ssem.at[0], sib_g, s).wait_recv()

    def fold_copy(part, block, ssem, gg, ss):
        rows = pl.ds(pl.multiple_of(part * 48, 16), 48)
        return pltpu.make_async_remote_copy(
            src_ref=fold_buf.at[block, rows],
            dst_ref=fold_buf.at[block, rows],
            send_sem=ssem,
            recv_sem=fold_rsem.at[part, block],
            device_id=(gg, ss),
            device_id_type=MESH,
        )

    def fold_out(d):
        return fold_copy(core, me, fold_ssem.at[d], g, seq_at(d))

    def fold_across(block):
        return fold_copy(core, block, fy_ssem.at[block % 8], y_g, y_s)

    def fold_sib(block):
        return fold_copy(core, block, fsib_ssem.at[block], sib_g, s)

    def fold_arrived(part, block):
        fold_copy(part, block, fold_ssem.at[0], sib_g, s).wait_recv()

    fold_across(me).start()
    for d in (4, 3, 5, 2, 6, 1, 7):
        fold_out(d).start()

    for load in load_o:
        load.wait()
    for first in firsts:
        first.start()
    across(me).start()

    load_lens.wait()

    def length(node):
        last = lens_ref.shape[0] - 1
        return jnp.where(node <= last, lens_ref[jnp.minimum(node, last)], 0)

    @pl.when(jnp.logical_not(low))
    def _():
        row = lax.broadcasted_iota(jnp.int32, (PACK, 128), 0)
        col = lax.broadcasted_iota(jnp.int32, (PACK, 128), 1)
        at = 64 * (15 - s) + row + 32 * (col // 64)
        for a in range(2):
            lat_early[a].wait_recv()
            lat_send[a] = jnp.where(
                at < length(2 * g + a), lat_next[a].astype(F32), lat_send[a].astype(F32)
            ).astype(BF)
        lat_sends(lambda c: c.start())

    lat_tok[main_at] = lat_send[y]

    def variance(xt):
        gx = dot(gram_buf[...], xt.astype(BF))
        return jnp.maximum(jnp.sum((gx[:64] + gx[64:]) * xt, axis=0, keepdims=True), 0.0)

    tail_len = length(2 * g + y)

    def at_step(n):
        turn = n % 4
        near = (z // 2 + jnp.where(turn < 2, turn, 5 - turn)) % 4
        return 8 * jnp.where(n < 4, y, 1 - y) + 2 * near

    def fold_relay(n):
        for h in range(2):
            block = at_step(n) + h

            @pl.when(block != me)
            def _():
                fold_arrived(core, block)

                @pl.when(n < 4)
                def _():
                    fold_across(block).start()

                fold_sib(block).start()

    def around(d, of):
        return [
            (of(d), d >= 0),
            (of(-d), jnp.logical_and(d != 0, d != 4)),
        ]

    def pass_on_z(i):
        d = jnp.where(i == 0, 2, jnp.where(i == 1, 1, i + 1))
        for block, there in around(d, column):

            @pl.when(there)
            def _():
                arrived(mine, block)
                across(block).start()
                to_x(block).start()
                to_sib(mine, block).start()

        @pl.when(i == 0)
        def _():
            on_up.start()
            on_down.start()
            on_far.start()

    def pass_on_y(i):
        d = jnp.where(i == 1, 2, jnp.where(i == 2, 1, i))
        for block, there in around(d, other):

            @pl.when(there)
            def _():
                arrived(mine, block)
                to_x(block).start()
                to_sib(mine, block).start()

    theirs = 2 * (1 - px) + core

    def pass_on_x(d, of):
        for block, there in around(d, of):

            @pl.when(there)
            def _():
                arrived(theirs, block)
                to_sib(theirs, block).start()

    for n in range(4):
        fold_relay(jnp.int32(n))
    pass_on_z(jnp.int32(0))
    pass_on_z(jnp.int32(1))

    @pl.loop(0, 16)
    def _(k):
        @pl.when(k != main_at)
        def _():
            lat_copy(lat_send.at[0], lat_tok.at[k], lat_ssem.at[0, 0], k, sib_g, s).wait_recv()

    head_lines = lat_tok[0:8].astype(F32).reshape(256, 128)
    tail_lines = lat_tok[8:16].astype(F32).reshape(256, 128)
    tokens = jnp.concatenate([unpacked(head_lines), unpacked(tail_lines)], axis=0)
    xt = tokens.T
    xkt[0:64, :] = jnp.zeros((64, 1024), BF)
    xkt[64:128, :] = xt.astype(BF)
    var = variance(xt)
    key_eps = 1e-6 * (var + 1e-5)
    scaled = xt * lax.rsqrt(var + 1e-5)
    extra = (lax.broadcasted_iota(jnp.int32, (64, 1024), 0) == 0).astype(F32)
    w = jnp.concatenate([scaled, extra], axis=0).T
    w_head[...] = w[:512].astype(BF)
    place = lax.broadcasted_iota(jnp.int32, (512, 128), 0)
    tail_spot = 64 * ((place % 256) // 32) + place % 32 + 32 * (place // 256)
    w_tail[:, :128] = w[512:].astype(BF)
    w_tail[:, 128:] = jnp.where(tail_spot < tail_len, w[512:], 0.0).astype(BF)

    q_tail = lat_tok[8 + tail_block].astype(F32)
    q_tok = jnp.concatenate([unpacked(lat_tok[head_block].astype(F32)), unpacked(q_tail)], axis=0)
    q_xt = q_tok.T
    q_eps = 1e-6 * (variance(q_xt) + 1e-5)
    q_xtz = jnp.concatenate([q_xt.astype(BF), jnp.zeros((64, 128), BF)], axis=0)
    q_side = lax.broadcasted_iota(jnp.int32, (128, 128), 1) < 64

    def rms(x, eps, scale):
        parts = []
        for h in range(2):
            rows = x[64 * h : 64 * h + 64]
            mean = jnp.sum(rows * rows, axis=0, keepdims=True) * (1.0 / HDIM)
            parts.append(rows * (lax.rsqrt(mean + eps) * scale))
        return jnp.concatenate(parts, axis=0)


    def prepare(n):
        first = at_step(n)
        for h in range(2):

            @pl.when(first + h != me)
            def _():
                fold_arrived(1 - core, first + h)

    def keys_of(n, turn):
        pair = fold_buf[pl.ds(at_step(n), 2), 0:64]
        pair_qk = jnp.concatenate([pair[0], pair[1]], axis=0)
        key_buf[turn] = rms(dot(pair_qk, xkt[...]), key_eps, 1.0).astype(BF)
        query = rms(dot(pair_qk, q_xtz), q_eps, QSCALE).T
        query_buf[turn] = jnp.concatenate(
            [jnp.where(q_side, query, 0.0), jnp.where(q_side, 0.0, query)], axis=0
        ).astype(BF)

    prepare(jnp.int32(0))
    keys_of(jnp.int32(0), 0)

    @pl.loop(0, 8)
    def _(n):
        @pl.when(n < 4)
        def _():
            fold_relay(n + 4)

        later = jnp.minimum(n + 1, 7)

        @pl.when(n < 7)
        def _():
            prepare(later)

        first = at_step(n)
        pair = fold_buf[pl.ds(first, 2)]
        query2 = query_buf[n % 2]
        keys_t = key_buf[n % 2]
        keys_of(later, (n + 1) % 2)
        p = jnp.exp2(dot(query2, keys_t)).astype(BF)
        u_head = dot(p[:, :512], w_head[...])
        u_tail = dot(p[:, 512:], w_tail[...])
        u_all = u_head + u_tail[:, :128]
        ratio = u_all[:, :64] / u_all[:, 64:65]
        u_over = jnp.concatenate([u_tail[64:128, 128:], u_tail[192:256, 128:]], axis=0)
        total = u_over[:, 64:65]
        over = u_over[:, :64] / jnp.where(total == 0.0, 1.0, total)
        mean_even = jnp.concatenate([ratio[:128], over[:64]], axis=0).astype(BF)
        mean_odd = jnp.concatenate([ratio[128:], over[64:]], axis=0).astype(BF)
        att_even = dot(mean_even, unpacked(pair[0, 64:96].astype(F32)).astype(BF))
        att_odd = dot(mean_odd, unpacked(pair[1, 64:96].astype(F32)).astype(BF))
        columns = pl.ds(pl.multiple_of(first * 64, 128), 128)
        att[:, columns] = jnp.concatenate([att_even, att_odd], axis=1).astype(BF)

        @pl.when(n < 2)
        def _():
            pass_on_z(n + 2)

        @pl.when(n < 5)
        def _():
            pass_on_y(n)

        @pl.when(jnp.logical_and(n >= 2, n < 6))
        def _():
            i = n - 2
            pass_on_x(jnp.where(i == 0, 2, jnp.where(i == 1, 1, i + 1)), column)


    tok2 = jnp.concatenate([q_tok, q_tok[64:]], axis=0).astype(BF)
    def project(part):
        columns = pl.ds(pl.multiple_of(part * quarter, 128), quarter)
        mix[:, columns] = dot(att[...], o_buf[part]) + dot(tok2, wi_ref[:, columns])

    def from_sib(part):
        @pl.loop(1, 16)
        def _(k):
            arrived(part, (me + k) % 16)

    project(mine)
    from_sib(2 * px + 1 - core)
    project(2 * px + 1 - core)
    for d in (0, 2, 1, 3, 4):
        pass_on_x(jnp.int32(d), other)
    project(theirs)
    from_sib(2 * (1 - px) + 1 - core)
    project(2 * (1 - px) + 1 - core)
    mixed = mix[...]
    mean = jnp.mean(mixed, axis=1, keepdims=True)
    centre = mixed - mean
    spread = jnp.mean(centre * centre, axis=1, keepdims=True)
    load_fgain.wait()
    load_ho.wait()
    final = (centre * lax.rsqrt(spread + 1e-5) * fgain_ref[...].reshape(1, -1)).astype(BF)
    score = dot_nt(final, ho_v[...])

    where_t = 64 * tail_block + lax.broadcasted_iota(jnp.int32, (64, 64), 0)
    counted = where_t < tail_len
    sc_send[0] = packed(score[:64])
    sc_send[1] = packed(jnp.where(counted, score[64:128] - score[128:], 0.0))
    turned = jnp.dot(
        reversal(),
        jnp.where(counted, 0.0, score[64:128]),
        precision=lax.Precision.HIGHEST,
        preferred_element_type=F32,
    )
    sc_send[2] = packed(turned)

    tail_g = jnp.where(y == 0, g, next_g)
    targets = [(g, head_block, y), (tail_g, tail_block, 3 - y), (g, 15 - tail_block, y)]

    def sc_copy(k, gg, ss, at):
        return pltpu.make_async_remote_copy(
            src_ref=sc_send.at[k],
            dst_ref=sc_recv.at[at],
            send_sem=sc_ssem.at[k],
            recv_sem=sc_rsem.at[at],
            device_id=(gg, ss),
            device_id_type=MESH,
        )

    own = [s == head_block, jnp.logical_and(y == 0, s == tail_block), s == 15 - tail_block]

    for k, (gg, ss, at) in enumerate(targets):

        @pl.when(jnp.logical_not(own[k]))
        def _():
            sc_copy(k, gg, ss, at).start()

        @pl.when(own[k])
        def _():
            sc_recv[at] = sc_send[k]

    lat_sends(lambda c: c.wait_send())

    @pl.when(low)
    def _():
        for early in lat_early:
            early.wait_send()

    @pl.loop(1, 16)
    def _(k):
        there = (me + k) % 16
        fold_sib(there).wait_send()
        to_x(there).wait_send()
        to_sib(mine, there).wait_send()
        to_sib(theirs, there).wait_send()

    @pl.loop(1, 8)
    def _(d):
        fold_out(d).wait_send()

    for sent in (*firsts, on_up, on_down, on_far):
        sent.wait_send()

    @pl.loop(0, 8)
    def _(k):
        across(8 * y + k).wait_send()
        fold_across(8 * y + k).wait_send()

    @pl.when(jnp.logical_not(low))
    def _():
        sc_recv[2] = jnp.zeros((PACK, 128), F32)
        sc_recv[3] = jnp.zeros((PACK, 128), F32)

    kept = jnp.logical_or(own[0], own[2])
    for a in range(2):

        @pl.when(jnp.logical_not(jnp.logical_and(kept, y == a)))
        def _():
            sc_copy(0, g, s, a).wait_recv()

    @pl.when(low)
    def _():
        sc_copy(0, g, s, 2).wait_recv()

        @pl.when(jnp.logical_not(own[1]))
        def _():
            sc_copy(0, g, s, 3).wait_recv()

    row = 64 * s + lax.broadcasted_iota(jnp.int32, (64, 64), 0)
    for a in range(2):
        slot = 2 * g + a
        gone = length(slot)
        step = lat_ref[a] + STEP * unpacked(sc_recv[a] + sc_recv[2 + a])
        out_ref[a] = jnp.where(row < 1024 - gone, step, 0.0)

    for k in range(3):

        @pl.when(jnp.logical_not(own[k]))
        def _():
            sc_copy(k, g, s, 0).wait_send()


def solution(mesh):
    groups = mesh.shape["group"]

    def body(latent, margin_len, in_weight, norm_gain, qkv_weight, out_weight, final_gain, head_out):
        width = in_weight.shape[1]
        vmem = pl.BlockSpec(memory_space=pltpu.VMEM)
        hbm = pl.BlockSpec(memory_space=pl.ANY)
        dma = pltpu.SemaphoreType.DMA
        return pl.pallas_call(
            functools.partial(kernel, groups),
            out_shape=jax.ShapeDtypeStruct(latent.shape, F32),
            in_specs=[hbm] * 8,
            out_specs=vmem,
            scratch_shapes=[
                pltpu.VMEM(latent.shape, F32),
                pltpu.SMEM(margin_len.shape, jnp.int32),
                pltpu.VMEM(in_weight.shape, BF),
                pltpu.VMEM((width,), F32),
                pltpu.VMEM((3, HDIM, width), BF),
                pltpu.VMEM((width,), F32),
                pltpu.VMEM(head_out.shape[::-1], BF),
                pltpu.VMEM((2, PACK, 128), BF),
                pltpu.VMEM((16, PACK, 128), BF),
                pltpu.VMEM((2, PACK, 128), BF),
                pltpu.VMEM((16, 96, 128), BF),
                pltpu.VMEM((128, HDIM), BF),
                pltpu.VMEM((4, 1024, width // 4), BF),
                pltpu.VMEM((128, 1024), BF),
                pltpu.VMEM((512, 128), BF),
                pltpu.VMEM((512, 256), BF),
                pltpu.VMEM((192, 1024), BF),
                pltpu.VMEM((192, width), F32),
                pltpu.VMEM((2, 128, 1024), BF),
                pltpu.VMEM((2, 256, 128), BF),
                pltpu.VMEM((3, PACK, 128), F32),
                pltpu.VMEM((4, PACK, 128), F32),
                dma((7,)),
                dma((4,)),
                dma((3, 8)),
                dma((24,)),
                dma((8,)),
                dma((8,)),
                dma((16,)),
                dma((2, 16)),
                dma((8,)),
                dma((8,)),
                dma((16,)),
                dma((2, 16)),
                dma((4, 16)),
                dma((3,)),
                dma((4,)),
            ],
            compiler_params=pltpu.CompilerParams(
                collective_id=0, has_side_effects=True, vmem_limit_bytes=60 * 1024 * 1024
            ),
        )(
            latent,
            margin_len,
            in_weight,
            norm_gain,
            jnp.swapaxes(qkv_weight, 1, 2),
            out_weight,
            final_gain,
            head_out.T,
        )

    in_specs = (
        P("group", "seq", None),
        P(),
        P(),
        P(),
        P(None, None, "seq"),
        P("seq", None),
        P(),
        P(),
    )
    return jax.shard_map(
        body, mesh=mesh, in_specs=in_specs, out_specs=P("group", "seq", None), check_vma=False
    )
```

```python
import functools
import math

import jax
import jax.numpy as jnp
from jax import lax
from jax.experimental import pallas as pl
from jax.experimental.pallas import tpu as pltpu
from jax.sharding import PartitionSpec as P

MESH = pl.DeviceIdType.MESH
BF = jnp.bfloat16
F32 = jnp.float32

HDIM = 64
STEP = -0.5
ROWS = 64
PACK = 32
QSCALE = HDIM**-0.5 * math.log2(math.e)


def dot(a, b):
    return jnp.dot(a, b, preferred_element_type=F32)


def dot_nt(a, b):
    return lax.dot_general(a, b, (((1,), (1,)), ((), ())), preferred_element_type=F32)


def hi_lo(x):
    hi = x.astype(BF)
    return hi, (x - hi.astype(F32)).astype(BF)


def packed(x):
    return jnp.concatenate([x[:PACK], x[PACK:]], axis=1)


def unpacked(x):
    return jnp.concatenate([x[:, :HDIM], x[:, HDIM:]], axis=0)


def reversal():
    r = lax.broadcasted_iota(jnp.int32, (ROWS, ROWS), 0)
    c = lax.broadcasted_iota(jnp.int32, (ROWS, ROWS), 1)
    return (r + c == ROWS - 1).astype(F32)


def kernel(
    groups,
    lat_hbm,
    lens_hbm,
    wi_hbm,
    gain_hbm,
    qkv_hbm,
    o_hbm,
    fgain_hbm,
    ho_hbm,
    out_ref,
    lat_ref,
    lens_ref,
    wi_ref,
    gain_ref,
    qkv_v,
    fgain_ref,
    ho_v,
    lat_send,
    lat_tok,
    lat_next,
    fold_buf,
    gram_buf,
    o_buf,
    xkt,
    w_head,
    w_tail,
    att,
    mix,
    key_buf,
    query_buf,
    sc_send,
    sc_recv,
    load_sem,
    own_sem,
    lat_ssem,
    lat_rsem,
    fold_ssem,
    fy_ssem,
    fsib_ssem,
    fold_rsem,
    z_ssem,
    y_ssem,
    x_ssem,
    sib_ssem,
    o_rsem,
    sc_ssem,
    sc_rsem,
):
    g = lax.axis_index("group")
    s = lax.axis_index("seq")
    z = s // 2
    y = s % 2
    core = g % 2
    prev_g = (g + groups - 1) % groups
    next_g = (g + 1) % groups
    sib_g = g + 1 - 2 * core
    y_g = (g + core * (groups // 2)) % groups
    y_s = 2 * z + 1 - y
    x = (g // 2) % 4
    px = x % 2
    x_step = jnp.where(core == 0, 1 - 2 * px, 2 * px - 1)
    x_g = g + 2 * ((x + x_step + 4) % 4 - x)
    mine = 2 * px + core
    me = 8 * y + z
    low = s < 8
    head_block = (z + 2) % 8
    tail_block = jnp.where(z < 4, 4 * (z // 2) + 2 * (1 - z % 2), (2 * z + 5) % 8)
    quarter = o_buf.shape[2]

    def block_rows(block):
        return pl.ds(pl.multiple_of(block * 64, 64), 64)

    load_lat, load_lens, load_wi, load_gain, load_qkv, load_fgain, load_ho = [
        pltpu.make_async_copy(src, dst, load_sem.at[k])
        for k, (src, dst) in enumerate(
            [
                (lat_hbm, lat_ref),
                (lens_hbm, lens_ref),
                (wi_hbm, wi_ref),
                (gain_hbm, gain_ref),
                (qkv_hbm, qkv_v),
                (fgain_hbm, fgain_ref),
                (ho_hbm, ho_v),
            ]
        )
    ]
    load_o = [
        pltpu.make_async_copy(
            o_hbm.at[:, pl.ds(k * quarter, quarter)], o_buf.at[k, block_rows(me)], own_sem.at[k]
        )
        for k in range(4)
    ]
    barrier = pltpu.get_barrier_semaphore()

    def greet(gg, ss):
        pl.semaphore_signal(barrier, inc=1, device_id=(gg, ss), device_id_type=MESH)

    @pl.loop(1, 16)
    def _(k):
        greet(g, (s + k) % 16)

    asker = jnp.where(
        s % 2 == 0, 2 * ((s % 8) // 4) + 1 - (s // 2) % 2, 4 + ((s + 3) % 8) // 2
    )
    greet(jnp.where(low, prev_g, next_g), 15 - s)

    @pl.when(low)
    def _():
        greet(prev_g, 2 * asker + 1)

    @pl.when(y == 1)
    def _():
        greet(next_g, tail_block)

    greet(sib_g, s)
    greet(x_g, s)

    @pl.when(core == 1)
    def _():
        greet(y_g, y_s)

    for load in [load_lat, load_wi, load_gain, load_qkv, *load_o, load_lens, load_fgain, load_ho]:
        load.start()

    flip = reversal().astype(BF)
    load_lat.wait()
    for a in range(2):
        rows = lat_ref[a].astype(BF)
        turned = jnp.where(low, rows.astype(F32), dot(flip, rows))
        lat_send[a] = packed(turned).astype(BF)

    def fold_weights():
        load_wi.wait()
        load_gain.wait()
        wi = wi_ref[...].astype(F32)
        centred = wi - jnp.mean(wi, axis=1, keepdims=True)
        wg_hi, wg_lo = hi_lo(centred * gain_ref[...].reshape(1, -1))
        wg = jnp.concatenate([wg_hi, wg_lo], axis=0)
        load_qkv.wait()
        fold2 = dot_nt(qkv_v[...].reshape(192, -1), wg)
        fold = fold2[:, :64] + fold2[:, 64:]
        fold_buf[me, 0:64] = jnp.concatenate([fold[:64], fold[64:128]], axis=1).astype(BF)
        fold_buf[me, 64:96] = packed(fold[128:].T).astype(BF)

        c_hi, c_lo = hi_lo(centred)
        cc = jnp.concatenate([c_hi, c_lo], axis=0)
        gram4 = dot_nt(cc, cc)
        gram2 = gram4[:64] + gram4[64:]
        gram_hi, gram_lo = hi_lo((gram2[:, :64] + gram2[:, 64:]) * (1.0 / wi.shape[1]))
        gram_buf[...] = jnp.concatenate([gram_hi, gram_lo], axis=0)

    fold_weights()

    n_greet = 18 + jnp.where(low, 1, 0) + y + core
    pl.semaphore_wait(barrier, n_greet)

    def lat_copy(src, dst, ssem, rsem, gg, ss):
        return pltpu.make_async_remote_copy(
            src_ref=src,
            dst_ref=dst,
            send_sem=ssem,
            recv_sem=lat_rsem.at[rsem],
            device_id=(gg, ss),
            device_id_type=MESH,
        )

    main_at = jnp.where(low, s, 23 - s)

    def lat_sends(act):
        @pl.loop(0, 8)
        def _(j):
            k = (z + j + 4) % 8
            for a in range(2):

                @pl.when(jnp.logical_not(jnp.logical_and(j == 4, y == a)))
                def _():
                    act(
                        lat_copy(
                            lat_send.at[a],
                            lat_tok.at[main_at],
                            lat_ssem.at[a, k],
                            main_at,
                            g,
                            2 * k + a,
                        )
                    )

    lat_early = [
        lat_copy(
            lat_send.at[1 - a],
            lat_next.at[a],
            lat_ssem.at[2, a],
            16 + a,
            g if a == 0 else prev_g,
            15 - s,
        )
        for a in range(2)
    ]

    @pl.when(low)
    def _():
        for early in lat_early:
            early.start()
        lat_sends(lambda c: c.start())

    def o_copy(part, block, ssem, gg, ss):
        return pltpu.make_async_remote_copy(
            src_ref=o_buf.at[part, block_rows(block)],
            dst_ref=o_buf.at[part, block_rows(block)],
            send_sem=ssem,
            recv_sem=o_rsem.at[part, block],
            device_id=(gg, ss),
            device_id_type=MESH,
        )

    def seq_at(d):
        return 2 * ((z + d + 8) % 8) + y

    def column(d):
        return 8 * y + (z + d + 8) % 8

    def other(d):
        return 8 * (1 - y) + (z + d + 8) % 8

    def along(k, d):
        return o_copy(mine, me, z_ssem.at[k], g, seq_at(d))

    firsts = [along(k, d) for k, d in enumerate((2, -2, 1, -1))]
    side = 1 - 2 * core
    on_up = o_copy(mine, column(-2), z_ssem.at[4], g, seq_at(1))
    on_down = o_copy(mine, column(2), z_ssem.at[5], g, seq_at(-1))
    on_far = o_copy(mine, column(-2 * side), z_ssem.at[6], g, seq_at(2 * side))

    def across(block):
        return o_copy(mine, block, y_ssem.at[block % 8], y_g, y_s)

    def to_x(block):
        return o_copy(mine, block, x_ssem.at[block], x_g, s)

    def to_sib(part, block):
        return o_copy(part, block, sib_ssem.at[part // 2, block], sib_g, s)

    def arrived(part, block):
        o_copy(part, block, z_ssem.at[0], sib_g, s).wait_recv()

    def fold_copy(part, block, ssem, gg, ss):
        rows = pl.ds(pl.multiple_of(part * 48, 16), 48)
        return pltpu.make_async_remote_copy(
            src_ref=fold_buf.at[block, rows],
            dst_ref=fold_buf.at[block, rows],
            send_sem=ssem,
            recv_sem=fold_rsem.at[part, block],
            device_id=(gg, ss),
            device_id_type=MESH,
        )

    def fold_out(d):
        return fold_copy(core, me, fold_ssem.at[d], g, seq_at(d))

    def fold_across(block):
        return fold_copy(core, block, fy_ssem.at[block % 8], y_g, y_s)

    def fold_sib(block):
        return fold_copy(core, block, fsib_ssem.at[block], sib_g, s)

    def fold_arrived(part, block):
        fold_copy(part, block, fold_ssem.at[0], sib_g, s).wait_recv()

    fold_across(me).start()
    for d in (4, 3, 5, 2, 6, 1, 7):
        fold_out(d).start()

    for load in load_o:
        load.wait()
    for first in firsts:
        first.start()
    across(me).start()

    load_lens.wait()

    def length(node):
        last = lens_ref.shape[0] - 1
        return jnp.where(node <= last, lens_ref[jnp.minimum(node, last)], 0)

    @pl.when(jnp.logical_not(low))
    def _():
        row = lax.broadcasted_iota(jnp.int32, (PACK, 128), 0)
        col = lax.broadcasted_iota(jnp.int32, (PACK, 128), 1)
        at = 64 * (15 - s) + row + 32 * (col // 64)
        for a in range(2):
            lat_early[a].wait_recv()
            lat_send[a] = jnp.where(
                at < length(2 * g + a), lat_next[a].astype(F32), lat_send[a].astype(F32)
            ).astype(BF)
        lat_sends(lambda c: c.start())

    lat_tok[main_at] = lat_send[y]

    def variance(xt):
        gx = dot(gram_buf[...], xt.astype(BF))
        return jnp.maximum(jnp.sum((gx[:64] + gx[64:]) * xt, axis=0, keepdims=True), 0.0)

    tail_len = length(2 * g + y)

    def at_step(n):
        turn = n % 4
        near = (z // 2 + jnp.where(turn < 2, turn, 5 - turn)) % 4
        return 8 * jnp.where(n < 4, y, 1 - y) + 2 * near

    def fold_relay(n):
        for h in range(2):
            block = at_step(n) + h

            @pl.when(block != me)
            def _():
                fold_arrived(core, block)

                @pl.when(n < 4)
                def _():
                    fold_across(block).start()

                fold_sib(block).start()

    def around(d, of):
        return [
            (of(d), d >= 0),
            (of(-d), jnp.logical_and(d != 0, d != 4)),
        ]

    def pass_on_z(i):
        d = jnp.where(i == 0, 2, jnp.where(i == 1, 1, i + 1))
        for block, there in around(d, column):

            @pl.when(there)
            def _():
                arrived(mine, block)
                across(block).start()
                to_x(block).start()
                to_sib(mine, block).start()

        @pl.when(i == 0)
        def _():
            on_up.start()
            on_down.start()
            on_far.start()

    def pass_on_y(i):
        d = jnp.where(i == 1, 2, jnp.where(i == 2, 1, i))
        for block, there in around(d, other):

            @pl.when(there)
            def _():
                arrived(mine, block)
                to_x(block).start()
                to_sib(mine, block).start()

    theirs = 2 * (1 - px) + core

    def pass_on_x(d, of):
        for block, there in around(d, of):

            @pl.when(there)
            def _():
                arrived(theirs, block)
                to_sib(theirs, block).start()

    for n in range(4):
        fold_relay(jnp.int32(n))
    pass_on_z(jnp.int32(0))
    pass_on_z(jnp.int32(1))

    @pl.loop(0, 16)
    def _(k):
        @pl.when(k != main_at)
        def _():
            lat_copy(lat_send.at[0], lat_tok.at[k], lat_ssem.at[0, 0], k, sib_g, s).wait_recv()

    head_lines = lat_tok[0:8].astype(F32).reshape(256, 128)
    tail_lines = lat_tok[8:16].astype(F32).reshape(256, 128)
    tokens = jnp.concatenate([unpacked(head_lines), unpacked(tail_lines)], axis=0)
    xt = tokens.T
    xkt[0:64, :] = jnp.zeros((64, 1024), BF)
    xkt[64:128, :] = xt.astype(BF)
    var = variance(xt)
    key_eps = 1e-6 * (var + 1e-5)
    scaled = xt * lax.rsqrt(var + 1e-5)
    extra = (lax.broadcasted_iota(jnp.int32, (64, 1024), 0) == 0).astype(F32)
    w = jnp.concatenate([scaled, extra], axis=0).T
    w_head[...] = w[:512].astype(BF)
    place = lax.broadcasted_iota(jnp.int32, (512, 128), 0)
    tail_spot = 64 * ((place % 256) // 32) + place % 32 + 32 * (place // 256)
    w_tail[:, :128] = w[512:].astype(BF)
    w_tail[:, 128:] = jnp.where(tail_spot < tail_len, w[512:], 0.0).astype(BF)

    q_tail = lat_tok[8 + tail_block].astype(F32)
    q_tok = jnp.concatenate([unpacked(lat_tok[head_block].astype(F32)), unpacked(q_tail)], axis=0)
    q_xt = q_tok.T
    q_eps = 1e-6 * (variance(q_xt) + 1e-5)
    q_xtz = jnp.concatenate([q_xt.astype(BF), jnp.zeros((64, 128), BF)], axis=0)
    q_side = lax.broadcasted_iota(jnp.int32, (128, 128), 1) < 64

    def rms(x, eps, scale):
        parts = []
        for h in range(2):
            rows = x[64 * h : 64 * h + 64]
            mean = jnp.sum(rows * rows, axis=0, keepdims=True) * (1.0 / HDIM)
            parts.append(rows * (lax.rsqrt(mean + eps) * scale))
        return jnp.concatenate(parts, axis=0)


    def prepare(n):
        first = at_step(n)
        for h in range(2):

            @pl.when(first + h != me)
            def _():
                fold_arrived(1 - core, first + h)

    def keys_of(n, turn):
        pair = fold_buf[pl.ds(at_step(n), 2), 0:64]
        pair_qk = jnp.concatenate([pair[0], pair[1]], axis=0)
        key_buf[turn] = rms(dot(pair_qk, xkt[...]), key_eps, 1.0).astype(BF)
        query = rms(dot(pair_qk, q_xtz), q_eps, QSCALE).T
        query_buf[turn] = jnp.concatenate(
            [jnp.where(q_side, query, 0.0), jnp.where(q_side, 0.0, query)], axis=0
        ).astype(BF)

    prepare(jnp.int32(0))
    keys_of(jnp.int32(0), 0)

    @pl.loop(0, 8)
    def _(n):
        @pl.when(n < 4)
        def _():
            fold_relay(n + 4)

        later = jnp.minimum(n + 1, 7)

        @pl.when(n < 7)
        def _():
            prepare(later)

        first = at_step(n)
        pair = fold_buf[pl.ds(first, 2)]
        query2 = query_buf[n % 2]
        keys_t = key_buf[n % 2]
        keys_of(later, (n + 1) % 2)
        p = jnp.exp2(dot(query2, keys_t)).astype(BF)
        u_head = dot(p[:, :512], w_head[...])
        u_tail = dot(p[:, 512:], w_tail[...])
        u_all = u_head + u_tail[:, :128]
        ratio = u_all[:, :64] / u_all[:, 64:65]
        u_over = jnp.concatenate([u_tail[64:128, 128:], u_tail[192:256, 128:]], axis=0)
        total = u_over[:, 64:65]
        over = u_over[:, :64] / jnp.where(total == 0.0, 1.0, total)
        mean_even = jnp.concatenate([ratio[:128], over[:64]], axis=0).astype(BF)
        mean_odd = jnp.concatenate([ratio[128:], over[64:]], axis=0).astype(BF)
        att_even = dot(mean_even, unpacked(pair[0, 64:96].astype(F32)).astype(BF))
        att_odd = dot(mean_odd, unpacked(pair[1, 64:96].astype(F32)).astype(BF))
        columns = pl.ds(pl.multiple_of(first * 64, 128), 128)
        att[:, columns] = jnp.concatenate([att_even, att_odd], axis=1).astype(BF)

        @pl.when(jnp.logical_and(n >= 1, n < 3))
        def _():
            pass_on_z(n + 1)

        @pl.when(jnp.logical_and(n >= 1, n < 6))
        def _():
            pass_on_y(n - 1)

        @pl.when(jnp.logical_and(n >= 3, n < 7))
        def _():
            i = n - 3
            pass_on_x(jnp.where(i == 0, 2, jnp.where(i == 1, 1, i + 1)), column)


    tok2 = jnp.concatenate([q_tok, q_tok[64:]], axis=0).astype(BF)
    def project(part):
        columns = pl.ds(pl.multiple_of(part * quarter, 128), quarter)
        mix[:, columns] = dot(att[...], o_buf[part]) + dot(tok2, wi_ref[:, columns])

    def from_sib(part):
        @pl.loop(1, 16)
        def _(k):
            arrived(part, (me + k) % 16)

    project(mine)
    from_sib(2 * px + 1 - core)
    project(2 * px + 1 - core)
    for d in (0, 2, 1, 3, 4):
        pass_on_x(jnp.int32(d), other)
    project(theirs)
    from_sib(2 * (1 - px) + 1 - core)
    project(2 * (1 - px) + 1 - core)
    mixed = mix[...]
    mean = jnp.mean(mixed, axis=1, keepdims=True)
    centre = mixed - mean
    spread = jnp.mean(centre * centre, axis=1, keepdims=True)
    load_fgain.wait()
    load_ho.wait()
    final = (centre * lax.rsqrt(spread + 1e-5) * fgain_ref[...].reshape(1, -1)).astype(BF)
    score = dot_nt(final, ho_v[...])

    where_t = 64 * tail_block + lax.broadcasted_iota(jnp.int32, (64, 64), 0)
    counted = where_t < tail_len
    sc_send[0] = packed(score[:64])
    sc_send[1] = packed(jnp.where(counted, score[64:128] - score[128:], 0.0))
    turned = jnp.dot(
        reversal(),
        jnp.where(counted, 0.0, score[64:128]),
        precision=lax.Precision.HIGHEST,
        preferred_element_type=F32,
    )
    sc_send[2] = packed(turned)

    tail_g = jnp.where(y == 0, g, next_g)
    targets = [(g, head_block, y), (tail_g, tail_block, 3 - y), (g, 15 - tail_block, y)]

    def sc_copy(k, gg, ss, at):
        return pltpu.make_async_remote_copy(
            src_ref=sc_send.at[k],
            dst_ref=sc_recv.at[at],
            send_sem=sc_ssem.at[k],
            recv_sem=sc_rsem.at[at],
            device_id=(gg, ss),
            device_id_type=MESH,
        )

    own = [s == head_block, jnp.logical_and(y == 0, s == tail_block), s == 15 - tail_block]

    for k, (gg, ss, at) in enumerate(targets):

        @pl.when(jnp.logical_not(own[k]))
        def _():
            sc_copy(k, gg, ss, at).start()

        @pl.when(own[k])
        def _():
            sc_recv[at] = sc_send[k]

    lat_sends(lambda c: c.wait_send())

    @pl.when(low)
    def _():
        for early in lat_early:
            early.wait_send()

    @pl.loop(1, 16)
    def _(k):
        there = (me + k) % 16
        fold_sib(there).wait_send()
        to_x(there).wait_send()
        to_sib(mine, there).wait_send()
        to_sib(theirs, there).wait_send()

    @pl.loop(1, 8)
    def _(d):
        fold_out(d).wait_send()

    for sent in (*firsts, on_up, on_down, on_far):
        sent.wait_send()

    @pl.loop(0, 8)
    def _(k):
        across(8 * y + k).wait_send()
        fold_across(8 * y + k).wait_send()

    @pl.when(jnp.logical_not(low))
    def _():
        sc_recv[2] = jnp.zeros((PACK, 128), F32)
        sc_recv[3] = jnp.zeros((PACK, 128), F32)

    kept = jnp.logical_or(own[0], own[2])
    for a in range(2):

        @pl.when(jnp.logical_not(jnp.logical_and(kept, y == a)))
        def _():
            sc_copy(0, g, s, a).wait_recv()

    @pl.when(low)
    def _():
        sc_copy(0, g, s, 2).wait_recv()

        @pl.when(jnp.logical_not(own[1]))
        def _():
            sc_copy(0, g, s, 3).wait_recv()

    row = 64 * s + lax.broadcasted_iota(jnp.int32, (64, 64), 0)
    for a in range(2):
        slot = 2 * g + a
        gone = length(slot)
        step = lat_ref[a] + STEP * unpacked(sc_recv[a] + sc_recv[2 + a])
        out_ref[a] = jnp.where(row < 1024 - gone, step, 0.0)

    for k in range(3):

        @pl.when(jnp.logical_not(own[k]))
        def _():
            sc_copy(k, g, s, 0).wait_send()


def solution(mesh):
    groups = mesh.shape["group"]

    def body(latent, margin_len, in_weight, norm_gain, qkv_weight, out_weight, final_gain, head_out):
        width = in_weight.shape[1]
        vmem = pl.BlockSpec(memory_space=pltpu.VMEM)
        hbm = pl.BlockSpec(memory_space=pl.ANY)
        dma = pltpu.SemaphoreType.DMA
        return pl.pallas_call(
            functools.partial(kernel, groups),
            out_shape=jax.ShapeDtypeStruct(latent.shape, F32),
            in_specs=[hbm] * 8,
            out_specs=vmem,
            scratch_shapes=[
                pltpu.VMEM(latent.shape, F32),
                pltpu.SMEM(margin_len.shape, jnp.int32),
                pltpu.VMEM(in_weight.shape, BF),
                pltpu.VMEM((width,), F32),
                pltpu.VMEM((3, HDIM, width), BF),
                pltpu.VMEM((width,), F32),
                pltpu.VMEM(head_out.shape[::-1], BF),
                pltpu.VMEM((2, PACK, 128), BF),
                pltpu.VMEM((16, PACK, 128), BF),
                pltpu.VMEM((2, PACK, 128), BF),
                pltpu.VMEM((16, 96, 128), BF),
                pltpu.VMEM((128, HDIM), BF),
                pltpu.VMEM((4, 1024, width // 4), BF),
                pltpu.VMEM((128, 1024), BF),
                pltpu.VMEM((512, 128), BF),
                pltpu.VMEM((512, 256), BF),
                pltpu.VMEM((192, 1024), BF),
                pltpu.VMEM((192, width), F32),
                pltpu.VMEM((2, 128, 1024), BF),
                pltpu.VMEM((2, 256, 128), BF),
                pltpu.VMEM((3, PACK, 128), F32),
                pltpu.VMEM((4, PACK, 128), F32),
                dma((7,)),
                dma((4,)),
                dma((3, 8)),
                dma((24,)),
                dma((8,)),
                dma((8,)),
                dma((16,)),
                dma((2, 16)),
                dma((8,)),
                dma((8,)),
                dma((16,)),
                dma((2, 16)),
                dma((4, 16)),
                dma((3,)),
                dma((4,)),
            ],
            compiler_params=pltpu.CompilerParams(
                collective_id=0, has_side_effects=True, vmem_limit_bytes=60 * 1024 * 1024
            ),
        )(
            latent,
            margin_len,
            in_weight,
            norm_gain,
            jnp.swapaxes(qkv_weight, 1, 2),
            out_weight,
            final_gain,
            head_out.T,
        )

    in_specs = (
        P("group", "seq", None),
        P(),
        P(),
        P(),
        P(None, None, "seq"),
        P("seq", None),
        P(),
        P(),
    )
    return jax.shard_map(
        body, mesh=mesh, in_specs=in_specs, out_specs=P("group", "seq", None), check_vma=False
    )
```

```python
import functools
import math

import jax
import jax.numpy as jnp
from jax import lax
from jax.experimental import pallas as pl
from jax.experimental.pallas import tpu as pltpu
from jax.sharding import PartitionSpec as P

MESH = pl.DeviceIdType.MESH
BF = jnp.bfloat16
F32 = jnp.float32

HDIM = 64
STEP = -0.5
ROWS = 64
PACK = 32
QSCALE = HDIM**-0.5 * math.log2(math.e)


def dot(a, b):
    return jnp.dot(a, b, preferred_element_type=F32)


def dot_nt(a, b):
    return lax.dot_general(a, b, (((1,), (1,)), ((), ())), preferred_element_type=F32)


def hi_lo(x):
    hi = x.astype(BF)
    return hi, (x - hi.astype(F32)).astype(BF)


def packed(x):
    return jnp.concatenate([x[:PACK], x[PACK:]], axis=1)


def unpacked(x):
    return jnp.concatenate([x[:, :HDIM], x[:, HDIM:]], axis=0)


def reversal():
    r = lax.broadcasted_iota(jnp.int32, (ROWS, ROWS), 0)
    c = lax.broadcasted_iota(jnp.int32, (ROWS, ROWS), 1)
    return (r + c == ROWS - 1).astype(F32)


def kernel(
    groups,
    lat_hbm,
    lens_hbm,
    wi_hbm,
    gain_hbm,
    qkv_hbm,
    o_hbm,
    fgain_hbm,
    ho_hbm,
    out_ref,
    lat_ref,
    lens_ref,
    wi_ref,
    gain_ref,
    qkv_v,
    fgain_ref,
    ho_v,
    lat_send,
    lat_tok,
    lat_next,
    fold_buf,
    gram_buf,
    o_buf,
    xkt,
    w_head,
    w_tail,
    att,
    mix,
    key_buf,
    query_buf,
    sc_send,
    sc_recv,
    load_sem,
    own_sem,
    lat_ssem,
    lat_rsem,
    fold_ssem,
    fy_ssem,
    fsib_ssem,
    fold_rsem,
    z_ssem,
    y_ssem,
    x_ssem,
    sib_ssem,
    o_rsem,
    sc_ssem,
    sc_rsem,
):
    g = lax.axis_index("group")
    s = lax.axis_index("seq")
    z = s // 2
    y = s % 2
    core = g % 2
    prev_g = (g + groups - 1) % groups
    next_g = (g + 1) % groups
    sib_g = g + 1 - 2 * core
    y_g = (g + core * (groups // 2)) % groups
    y_s = 2 * z + 1 - y
    x = (g // 2) % 4
    px = x % 2
    x_step = jnp.where(core == 0, 1 - 2 * px, 2 * px - 1)
    x_g = g + 2 * ((x + x_step + 4) % 4 - x)
    mine = 2 * px + core
    me = 8 * y + z
    low = s < 8
    head_block = (z + 2) % 8
    tail_block = jnp.where(z < 4, 4 * (z // 2) + 2 * (1 - z % 2), (2 * z + 5) % 8)
    quarter = o_buf.shape[2]

    def block_rows(block):
        return pl.ds(pl.multiple_of(block * 64, 64), 64)

    load_lat, load_lens, load_wi, load_gain, load_qkv, load_fgain, load_ho = [
        pltpu.make_async_copy(src, dst, load_sem.at[k])
        for k, (src, dst) in enumerate(
            [
                (lat_hbm, lat_ref),
                (lens_hbm, lens_ref),
                (wi_hbm, wi_ref),
                (gain_hbm, gain_ref),
                (qkv_hbm, qkv_v),
                (fgain_hbm, fgain_ref),
                (ho_hbm, ho_v),
            ]
        )
    ]
    load_o = [
        pltpu.make_async_copy(
            o_hbm.at[:, pl.ds(k * quarter, quarter)], o_buf.at[k, block_rows(me)], own_sem.at[k]
        )
        for k in range(4)
    ]
    barrier = pltpu.get_barrier_semaphore()

    def greet(gg, ss):
        pl.semaphore_signal(barrier, inc=1, device_id=(gg, ss), device_id_type=MESH)

    @pl.loop(1, 16)
    def _(k):
        greet(g, (s + k) % 16)

    asker = jnp.where(
        s % 2 == 0, 2 * ((s % 8) // 4) + 1 - (s // 2) % 2, 4 + ((s + 3) % 8) // 2
    )
    greet(jnp.where(low, prev_g, next_g), 15 - s)

    @pl.when(low)
    def _():
        greet(prev_g, 2 * asker + 1)

    @pl.when(y == 1)
    def _():
        greet(next_g, tail_block)

    greet(sib_g, s)
    greet(x_g, s)

    @pl.when(core == 1)
    def _():
        greet(y_g, y_s)

    for load in [load_lat, load_wi, load_gain, load_qkv, *load_o, load_lens, load_fgain, load_ho]:
        load.start()

    flip = reversal().astype(BF)
    load_lat.wait()
    for a in range(2):
        rows = lat_ref[a].astype(BF)
        turned = jnp.where(low, rows.astype(F32), dot(flip, rows))
        lat_send[a] = packed(turned).astype(BF)

    def fold_weights():
        load_wi.wait()
        load_gain.wait()
        wi = wi_ref[...].astype(F32)
        centred = wi - jnp.mean(wi, axis=1, keepdims=True)
        wg_hi, wg_lo = hi_lo(centred * gain_ref[...].reshape(1, -1))
        wg = jnp.concatenate([wg_hi, wg_lo], axis=0)
        load_qkv.wait()
        fold2 = dot_nt(qkv_v[...].reshape(192, -1), wg)
        fold = fold2[:, :64] + fold2[:, 64:]
        fold_buf[me, 0:64] = jnp.concatenate([fold[:64], fold[64:128]], axis=1).astype(BF)
        fold_buf[me, 64:96] = packed(fold[128:].T).astype(BF)

        c_hi, c_lo = hi_lo(centred)
        cc = jnp.concatenate([c_hi, c_lo], axis=0)
        gram4 = dot_nt(cc, cc)
        gram2 = gram4[:64] + gram4[64:]
        gram_hi, gram_lo = hi_lo((gram2[:, :64] + gram2[:, 64:]) * (1.0 / wi.shape[1]))
        gram_buf[...] = jnp.concatenate([gram_hi, gram_lo], axis=0)

    fold_weights()

    n_greet = 18 + jnp.where(low, 1, 0) + y + core
    pl.semaphore_wait(barrier, n_greet)

    def lat_copy(src, dst, ssem, rsem, gg, ss):
        return pltpu.make_async_remote_copy(
            src_ref=src,
            dst_ref=dst,
            send_sem=ssem,
            recv_sem=lat_rsem.at[rsem],
            device_id=(gg, ss),
            device_id_type=MESH,
        )

    main_at = jnp.where(low, s, 23 - s)

    def lat_sends(act):
        @pl.loop(0, 8)
        def _(j):
            k = (z + j + 4) % 8
            for a in range(2):

                @pl.when(jnp.logical_not(jnp.logical_and(j == 4, y == a)))
                def _():
                    act(
                        lat_copy(
                            lat_send.at[a],
                            lat_tok.at[main_at],
                            lat_ssem.at[a, k],
                            main_at,
                            g,
                            2 * k + a,
                        )
                    )

    lat_early = [
        lat_copy(
            lat_send.at[1 - a],
            lat_next.at[a],
            lat_ssem.at[2, a],
            16 + a,
            g if a == 0 else prev_g,
            15 - s,
        )
        for a in range(2)
    ]

    @pl.when(low)
    def _():
        for early in lat_early:
            early.start()
        lat_sends(lambda c: c.start())

    def o_copy(part, block, ssem, gg, ss):
        return pltpu.make_async_remote_copy(
            src_ref=o_buf.at[part, block_rows(block)],
            dst_ref=o_buf.at[part, block_rows(block)],
            send_sem=ssem,
            recv_sem=o_rsem.at[part, block],
            device_id=(gg, ss),
            device_id_type=MESH,
        )

    def seq_at(d):
        return 2 * ((z + d + 8) % 8) + y

    def column(d):
        return 8 * y + (z + d + 8) % 8

    def other(d):
        return 8 * (1 - y) + (z + d + 8) % 8

    def along(k, d):
        return o_copy(mine, me, z_ssem.at[k], g, seq_at(d))

    firsts = [along(k, d) for k, d in enumerate((2, -2, 1, -1))]
    side = 1 - 2 * core
    on_up = o_copy(mine, column(-2), z_ssem.at[4], g, seq_at(1))
    on_down = o_copy(mine, column(2), z_ssem.at[5], g, seq_at(-1))
    on_far = o_copy(mine, column(-2 * side), z_ssem.at[6], g, seq_at(2 * side))

    def across(block):
        return o_copy(mine, block, y_ssem.at[block % 8], y_g, y_s)

    def to_x(block):
        return o_copy(mine, block, x_ssem.at[block], x_g, s)

    def to_sib(part, block):
        return o_copy(part, block, sib_ssem.at[part // 2, block], sib_g, s)

    def arrived(part, block):
        o_copy(part, block, z_ssem.at[0], sib_g, s).wait_recv()

    def fold_copy(part, block, ssem, gg, ss):
        rows = pl.ds(pl.multiple_of(part * 48, 16), 48)
        return pltpu.make_async_remote_copy(
            src_ref=fold_buf.at[block, rows],
            dst_ref=fold_buf.at[block, rows],
            send_sem=ssem,
            recv_sem=fold_rsem.at[part, block],
            device_id=(gg, ss),
            device_id_type=MESH,
        )

    def fold_out(d):
        return fold_copy(core, me, fold_ssem.at[d], g, seq_at(d))

    def fold_across(block):
        return fold_copy(core, block, fy_ssem.at[block % 8], y_g, y_s)

    def fold_sib(block):
        return fold_copy(core, block, fsib_ssem.at[block], sib_g, s)

    def fold_arrived(part, block):
        fold_copy(part, block, fold_ssem.at[0], sib_g, s).wait_recv()

    fold_across(me).start()
    for d in (4, 3, 5, 2, 6, 1, 7):
        fold_out(d).start()

    for load in load_o:
        load.wait()
    for first in firsts:
        first.start()
    across(me).start()

    load_lens.wait()

    def length(node):
        last = lens_ref.shape[0] - 1
        return jnp.where(node <= last, lens_ref[jnp.minimum(node, last)], 0)

    @pl.when(jnp.logical_not(low))
    def _():
        row = lax.broadcasted_iota(jnp.int32, (PACK, 128), 0)
        col = lax.broadcasted_iota(jnp.int32, (PACK, 128), 1)
        at = 64 * (15 - s) + row + 32 * (col // 64)
        for a in range(2):
            lat_early[a].wait_recv()
            lat_send[a] = jnp.where(
                at < length(2 * g + a), lat_next[a].astype(F32), lat_send[a].astype(F32)
            ).astype(BF)
        lat_sends(lambda c: c.start())

    lat_tok[main_at] = lat_send[y]

    def variance(xt):
        gx = dot(gram_buf[...], xt.astype(BF))
        return jnp.maximum(jnp.sum((gx[:64] + gx[64:]) * xt, axis=0, keepdims=True), 0.0)

    tail_len = length(2 * g + y)

    def at_step(n):
        turn = n % 4
        near = (z // 2 + jnp.where(turn < 2, turn, 5 - turn)) % 4
        return 8 * jnp.where(n < 4, y, 1 - y) + 2 * near

    def fold_relay(n):
        for h in range(2):
            block = at_step(n) + h

            @pl.when(block != me)
            def _():
                fold_arrived(core, block)

                @pl.when(n < 4)
                def _():
                    fold_across(block).start()

                fold_sib(block).start()

    def around(d, of):
        return [
            (of(d), d >= 0),
            (of(-d), jnp.logical_and(d != 0, d != 4)),
        ]

    def pass_on_z(i):
        d = jnp.where(i == 0, 2, jnp.where(i == 1, 1, i + 1))
        for block, there in around(d, column):

            @pl.when(there)
            def _():
                arrived(mine, block)
                across(block).start()
                to_x(block).start()
                to_sib(mine, block).start()

        @pl.when(i == 0)
        def _():
            on_up.start()
            on_down.start()
            on_far.start()

    def pass_on_y(i):
        d = jnp.where(i == 1, 2, jnp.where(i == 2, 1, i))
        for block, there in around(d, other):

            @pl.when(there)
            def _():
                arrived(mine, block)
                to_x(block).start()
                to_sib(mine, block).start()

    theirs = 2 * (1 - px) + core

    def pass_on_x(d, of):
        for block, there in around(d, of):

            @pl.when(there)
            def _():
                arrived(theirs, block)
                to_sib(theirs, block).start()

    for n in range(4):
        fold_relay(jnp.int32(n))
    pass_on_z(jnp.int32(0))
    pass_on_z(jnp.int32(1))

    @pl.loop(0, 16)
    def _(k):
        @pl.when(k != main_at)
        def _():
            lat_copy(lat_send.at[0], lat_tok.at[k], lat_ssem.at[0, 0], k, sib_g, s).wait_recv()

    head_lines = lat_tok[0:8].astype(F32).reshape(256, 128)
    tail_lines = lat_tok[8:16].astype(F32).reshape(256, 128)
    tokens = jnp.concatenate([unpacked(head_lines), unpacked(tail_lines)], axis=0)
    xt = tokens.T
    xkt[0:64, :] = jnp.zeros((64, 1024), BF)
    xkt[64:128, :] = xt.astype(BF)
    var = variance(xt)
    key_eps = 1e-6 * (var + 1e-5)
    scaled = xt * lax.rsqrt(var + 1e-5)
    extra = (lax.broadcasted_iota(jnp.int32, (64, 1024), 0) == 0).astype(F32)
    w = jnp.concatenate([scaled, extra], axis=0).T
    w_head[...] = w[:512].astype(BF)
    place = lax.broadcasted_iota(jnp.int32, (512, 128), 0)
    tail_spot = 64 * ((place % 256) // 32) + place % 32 + 32 * (place // 256)
    w_tail[:, :128] = w[512:].astype(BF)
    w_tail[:, 128:] = jnp.where(tail_spot < tail_len, w[512:], 0.0).astype(BF)

    q_tail = lat_tok[8 + tail_block].astype(F32)
    q_tok = jnp.concatenate([unpacked(lat_tok[head_block].astype(F32)), unpacked(q_tail)], axis=0)
    q_xt = q_tok.T
    q_eps = 1e-6 * (variance(q_xt) + 1e-5)
    q_xtz = jnp.concatenate([q_xt.astype(BF), jnp.zeros((64, 128), BF)], axis=0)
    q_side = lax.broadcasted_iota(jnp.int32, (128, 128), 1) < 64

    def rms(x, eps, scale):
        parts = []
        for h in range(2):
            rows = x[64 * h : 64 * h + 64]
            mean = jnp.sum(rows * rows, axis=0, keepdims=True) * (1.0 / HDIM)
            parts.append(rows * (lax.rsqrt(mean + eps) * scale))
        return jnp.concatenate(parts, axis=0)


    def prepare(n):
        first = at_step(n)
        for h in range(2):

            @pl.when(first + h != me)
            def _():
                fold_arrived(1 - core, first + h)

    def keys_of(n, turn):
        pair = fold_buf[pl.ds(at_step(n), 2), 0:64]
        pair_qk = jnp.concatenate([pair[0], pair[1]], axis=0)
        key_buf[turn] = rms(dot(pair_qk, xkt[...]), key_eps, 1.0).astype(BF)
        query = rms(dot(pair_qk, q_xtz), q_eps, QSCALE).T
        query_buf[turn] = jnp.concatenate(
            [jnp.where(q_side, query, 0.0), jnp.where(q_side, 0.0, query)], axis=0
        ).astype(BF)

    prepare(jnp.int32(0))
    keys_of(jnp.int32(0), 0)

    @pl.loop(0, 8)
    def _(n):
        @pl.when(n < 4)
        def _():
            fold_relay(n + 4)

        later = jnp.minimum(n + 1, 7)

        @pl.when(n < 7)
        def _():
            prepare(later)

        first = at_step(n)
        pair = fold_buf[pl.ds(first, 2)]
        query2 = query_buf[n % 2]
        keys_t = key_buf[n % 2]
        keys_of(later, (n + 1) % 2)
        p = jnp.exp2(dot(query2, keys_t)).astype(BF)
        u_head = dot(p[:, :512], w_head[...])
        u_tail = dot(p[:, 512:], w_tail[...])
        u_all = u_head + u_tail[:, :128]
        ratio = u_all[:, :64] / u_all[:, 64:65]
        u_over = jnp.concatenate([u_tail[64:128, 128:], u_tail[192:256, 128:]], axis=0)
        total = u_over[:, 64:65]
        over = u_over[:, :64] / jnp.where(total == 0.0, 1.0, total)
        mean_even = jnp.concatenate([ratio[:128], over[:64]], axis=0).astype(BF)
        mean_odd = jnp.concatenate([ratio[128:], over[64:]], axis=0).astype(BF)
        att_even = dot(mean_even, unpacked(pair[0, 64:96].astype(F32)).astype(BF))
        att_odd = dot(mean_odd, unpacked(pair[1, 64:96].astype(F32)).astype(BF))
        columns = pl.ds(pl.multiple_of(first * 64, 128), 128)
        att[:, columns] = jnp.concatenate([att_even, att_odd], axis=1).astype(BF)

        @pl.when(jnp.logical_and(n >= 1, n < 3))
        def _():
            pass_on_z(n + 1)

        @pl.when(jnp.logical_and(n >= 1, n < 6))
        def _():
            pass_on_y(n - 1)

        @pl.when(jnp.logical_and(n >= 3, n < 7))
        def _():
            i = n - 3
            pass_on_x(jnp.where(i == 0, 2, jnp.where(i == 1, 1, i + 1)), column)


    tok2 = jnp.concatenate([q_tok, q_tok[64:]], axis=0).astype(BF)
    def project(part):
        columns = pl.ds(pl.multiple_of(part * quarter, 128), quarter)
        mix[:, columns] = dot(att[...], o_buf[part]) + dot(tok2, wi_ref[:, columns])

    def from_sib(part):
        @pl.loop(1, 16)
        def _(k):
            arrived(part, (me + k) % 16)

    for d in (0, 2, 1, 3, 4):
        pass_on_x(jnp.int32(d), other)
    project(mine)
    from_sib(2 * px + 1 - core)
    project(2 * px + 1 - core)
    project(theirs)
    from_sib(2 * (1 - px) + 1 - core)
    project(2 * (1 - px) + 1 - core)
    mixed = mix[...]
    mean = jnp.mean(mixed, axis=1, keepdims=True)
    centre = mixed - mean
    spread = jnp.mean(centre * centre, axis=1, keepdims=True)
    load_fgain.wait()
    load_ho.wait()
    final = (centre * lax.rsqrt(spread + 1e-5) * fgain_ref[...].reshape(1, -1)).astype(BF)
    score = dot_nt(final, ho_v[...])

    where_t = 64 * tail_block + lax.broadcasted_iota(jnp.int32, (64, 64), 0)
    counted = where_t < tail_len
    sc_send[0] = packed(score[:64])
    sc_send[1] = packed(jnp.where(counted, score[64:128] - score[128:], 0.0))
    turned = jnp.dot(
        reversal(),
        jnp.where(counted, 0.0, score[64:128]),
        precision=lax.Precision.HIGHEST,
        preferred_element_type=F32,
    )
    sc_send[2] = packed(turned)

    tail_g = jnp.where(y == 0, g, next_g)
    targets = [(g, head_block, y), (tail_g, tail_block, 3 - y), (g, 15 - tail_block, y)]

    def sc_copy(k, gg, ss, at):
        return pltpu.make_async_remote_copy(
            src_ref=sc_send.at[k],
            dst_ref=sc_recv.at[at],
            send_sem=sc_ssem.at[k],
            recv_sem=sc_rsem.at[at],
            device_id=(gg, ss),
            device_id_type=MESH,
        )

    own = [s == head_block, jnp.logical_and(y == 0, s == tail_block), s == 15 - tail_block]

    for k, (gg, ss, at) in enumerate(targets):

        @pl.when(jnp.logical_not(own[k]))
        def _():
            sc_copy(k, gg, ss, at).start()

        @pl.when(own[k])
        def _():
            sc_recv[at] = sc_send[k]

    lat_sends(lambda c: c.wait_send())

    @pl.when(low)
    def _():
        for early in lat_early:
            early.wait_send()

    @pl.loop(1, 16)
    def _(k):
        there = (me + k) % 16
        fold_sib(there).wait_send()
        to_x(there).wait_send()
        to_sib(mine, there).wait_send()
        to_sib(theirs, there).wait_send()

    @pl.loop(1, 8)
    def _(d):
        fold_out(d).wait_send()

    for sent in (*firsts, on_up, on_down, on_far):
        sent.wait_send()

    @pl.loop(0, 8)
    def _(k):
        across(8 * y + k).wait_send()
        fold_across(8 * y + k).wait_send()

    @pl.when(jnp.logical_not(low))
    def _():
        sc_recv[2] = jnp.zeros((PACK, 128), F32)
        sc_recv[3] = jnp.zeros((PACK, 128), F32)

    kept = jnp.logical_or(own[0], own[2])
    for a in range(2):

        @pl.when(jnp.logical_not(jnp.logical_and(kept, y == a)))
        def _():
            sc_copy(0, g, s, a).wait_recv()

    @pl.when(low)
    def _():
        sc_copy(0, g, s, 2).wait_recv()

        @pl.when(jnp.logical_not(own[1]))
        def _():
            sc_copy(0, g, s, 3).wait_recv()

    row = 64 * s + lax.broadcasted_iota(jnp.int32, (64, 64), 0)
    for a in range(2):
        slot = 2 * g + a
        gone = length(slot)
        step = lat_ref[a] + STEP * unpacked(sc_recv[a] + sc_recv[2 + a])
        out_ref[a] = jnp.where(row < 1024 - gone, step, 0.0)

    for k in range(3):

        @pl.when(jnp.logical_not(own[k]))
        def _():
            sc_copy(k, g, s, 0).wait_send()


def solution(mesh):
    groups = mesh.shape["group"]

    def body(latent, margin_len, in_weight, norm_gain, qkv_weight, out_weight, final_gain, head_out):
        width = in_weight.shape[1]
        vmem = pl.BlockSpec(memory_space=pltpu.VMEM)
        hbm = pl.BlockSpec(memory_space=pl.ANY)
        dma = pltpu.SemaphoreType.DMA
        return pl.pallas_call(
            functools.partial(kernel, groups),
            out_shape=jax.ShapeDtypeStruct(latent.shape, F32),
            in_specs=[hbm] * 8,
            out_specs=vmem,
            scratch_shapes=[
                pltpu.VMEM(latent.shape, F32),
                pltpu.SMEM(margin_len.shape, jnp.int32),
                pltpu.VMEM(in_weight.shape, BF),
                pltpu.VMEM((width,), F32),
                pltpu.VMEM((3, HDIM, width), BF),
                pltpu.VMEM((width,), F32),
                pltpu.VMEM(head_out.shape[::-1], BF),
                pltpu.VMEM((2, PACK, 128), BF),
                pltpu.VMEM((16, PACK, 128), BF),
                pltpu.VMEM((2, PACK, 128), BF),
                pltpu.VMEM((16, 96, 128), BF),
                pltpu.VMEM((128, HDIM), BF),
                pltpu.VMEM((4, 1024, width // 4), BF),
                pltpu.VMEM((128, 1024), BF),
                pltpu.VMEM((512, 128), BF),
                pltpu.VMEM((512, 256), BF),
                pltpu.VMEM((192, 1024), BF),
                pltpu.VMEM((192, width), F32),
                pltpu.VMEM((2, 128, 1024), BF),
                pltpu.VMEM((2, 256, 128), BF),
                pltpu.VMEM((3, PACK, 128), F32),
                pltpu.VMEM((4, PACK, 128), F32),
                dma((7,)),
                dma((4,)),
                dma((3, 8)),
                dma((24,)),
                dma((8,)),
                dma((8,)),
                dma((16,)),
                dma((2, 16)),
                dma((8,)),
                dma((8,)),
                dma((16,)),
                dma((2, 16)),
                dma((4, 16)),
                dma((3,)),
                dma((4,)),
            ],
            compiler_params=pltpu.CompilerParams(
                collective_id=0, has_side_effects=True, vmem_limit_bytes=60 * 1024 * 1024
            ),
        )(
            latent,
            margin_len,
            in_weight,
            norm_gain,
            jnp.swapaxes(qkv_weight, 1, 2),
            out_weight,
            final_gain,
            head_out.T,
        )

    in_specs = (
        P("group", "seq", None),
        P(),
        P(),
        P(),
        P(None, None, "seq"),
        P("seq", None),
        P(),
        P(),
    )
    return jax.shard_map(
        body, mesh=mesh, in_specs=in_specs, out_specs=P("group", "seq", None), check_vma=False
    )
```

```python
import functools
import math

import jax
import jax.numpy as jnp
from jax import lax
from jax.experimental import pallas as pl
from jax.experimental.pallas import tpu as pltpu
from jax.sharding import PartitionSpec as P

MESH = pl.DeviceIdType.MESH
BF = jnp.bfloat16
F32 = jnp.float32

HDIM = 64
STEP = -0.5
ROWS = 64
PACK = 32
QSCALE = HDIM**-0.5 * math.log2(math.e)


def dot(a, b):
    return jnp.dot(a, b, preferred_element_type=F32)


def dot_nt(a, b):
    return lax.dot_general(a, b, (((1,), (1,)), ((), ())), preferred_element_type=F32)


def hi_lo(x):
    hi = x.astype(BF)
    return hi, (x - hi.astype(F32)).astype(BF)


def packed(x):
    return jnp.concatenate([x[:PACK], x[PACK:]], axis=1)


def unpacked(x):
    return jnp.concatenate([x[:, :HDIM], x[:, HDIM:]], axis=0)


def reversal():
    r = lax.broadcasted_iota(jnp.int32, (ROWS, ROWS), 0)
    c = lax.broadcasted_iota(jnp.int32, (ROWS, ROWS), 1)
    return (r + c == ROWS - 1).astype(F32)


def kernel(
    groups,
    lat_hbm,
    lens_hbm,
    wi_hbm,
    gain_hbm,
    qkv_hbm,
    o_hbm,
    fgain_hbm,
    ho_hbm,
    out_ref,
    lat_ref,
    lens_ref,
    wi_ref,
    gain_ref,
    qkv_v,
    fgain_ref,
    ho_v,
    lat_send,
    lat_tok,
    lat_next,
    fold_buf,
    gram_buf,
    o_buf,
    xkt,
    w_head,
    w_tail,
    att,
    mix,
    key_buf,
    query_buf,
    sc_send,
    sc_recv,
    load_sem,
    own_sem,
    lat_ssem,
    lat_rsem,
    fold_ssem,
    fy_ssem,
    fsib_ssem,
    fold_rsem,
    z_ssem,
    y_ssem,
    x_ssem,
    sib_ssem,
    o_rsem,
    sc_ssem,
    sc_rsem,
):
    g = lax.axis_index("group")
    s = lax.axis_index("seq")
    z = s // 2
    y = s % 2
    core = g % 2
    prev_g = (g + groups - 1) % groups
    next_g = (g + 1) % groups
    sib_g = g + 1 - 2 * core
    y_g = (g + core * (groups // 2)) % groups
    y_s = 2 * z + 1 - y
    x = (g // 2) % 4
    px = x % 2
    x_step = jnp.where(core == 0, 1 - 2 * px, 2 * px - 1)
    x_g = g + 2 * ((x + x_step + 4) % 4 - x)
    mine = 2 * px + core
    me = 8 * y + z
    low = s < 8
    head_block = (z + 2) % 8
    tail_block = jnp.where(z < 4, 4 * (z // 2) + 2 * (1 - z % 2), (2 * z + 5) % 8)
    quarter = o_buf.shape[2]

    def block_rows(block):
        return pl.ds(pl.multiple_of(block * 64, 64), 64)

    load_lat, load_lens, load_wi, load_gain, load_qkv, load_fgain, load_ho = [
        pltpu.make_async_copy(src, dst, load_sem.at[k])
        for k, (src, dst) in enumerate(
            [
                (lat_hbm, lat_ref),
                (lens_hbm, lens_ref),
                (wi_hbm, wi_ref),
                (gain_hbm, gain_ref),
                (qkv_hbm, qkv_v),
                (fgain_hbm, fgain_ref),
                (ho_hbm, ho_v),
            ]
        )
    ]
    load_o = [
        pltpu.make_async_copy(
            o_hbm.at[:, pl.ds(k * quarter, quarter)], o_buf.at[k, block_rows(me)], own_sem.at[k]
        )
        for k in range(4)
    ]
    barrier = pltpu.get_barrier_semaphore()

    def greet(gg, ss):
        pl.semaphore_signal(barrier, inc=1, device_id=(gg, ss), device_id_type=MESH)

    @pl.loop(1, 16)
    def _(k):
        greet(g, (s + k) % 16)

    asker = jnp.where(
        s % 2 == 0, 2 * ((s % 8) // 4) + 1 - (s // 2) % 2, 4 + ((s + 3) % 8) // 2
    )
    greet(jnp.where(low, prev_g, next_g), 15 - s)

    @pl.when(low)
    def _():
        greet(prev_g, 2 * asker + 1)

    @pl.when(y == 1)
    def _():
        greet(next_g, tail_block)

    greet(sib_g, s)
    greet(x_g, s)

    @pl.when(core == 1)
    def _():
        greet(y_g, y_s)

    for load in [load_lat, load_wi, load_gain, load_qkv, *load_o, load_lens, load_fgain, load_ho]:
        load.start()

    flip = reversal().astype(BF)
    load_lat.wait()
    for a in range(2):
        rows = lat_ref[a].astype(BF)
        turned = jnp.where(low, rows.astype(F32), dot(flip, rows))
        lat_send[a] = packed(turned).astype(BF)

    def fold_weights():
        load_wi.wait()
        load_gain.wait()
        wi = wi_ref[...].astype(F32)
        centred = wi - jnp.mean(wi, axis=1, keepdims=True)
        wg_hi, wg_lo = hi_lo(centred * gain_ref[...].reshape(1, -1))
        wg = jnp.concatenate([wg_hi, wg_lo], axis=0)
        load_qkv.wait()
        fold2 = dot_nt(qkv_v[...].reshape(192, -1), wg)
        fold = fold2[:, :64] + fold2[:, 64:]
        fold_buf[me, 0:64] = jnp.concatenate([fold[:64], fold[64:128]], axis=1).astype(BF)
        fold_buf[me, 64:96] = packed(fold[128:].T).astype(BF)

        c_hi, c_lo = hi_lo(centred)
        cc = jnp.concatenate([c_hi, c_lo], axis=0)
        gram4 = dot_nt(cc, cc)
        gram2 = gram4[:64] + gram4[64:]
        gram_hi, gram_lo = hi_lo((gram2[:, :64] + gram2[:, 64:]) * (1.0 / wi.shape[1]))
        gram_buf[...] = jnp.concatenate([gram_hi, gram_lo], axis=0)

    fold_weights()

    n_greet = 18 + jnp.where(low, 1, 0) + y + core
    pl.semaphore_wait(barrier, n_greet)

    def lat_copy(src, dst, ssem, rsem, gg, ss):
        return pltpu.make_async_remote_copy(
            src_ref=src,
            dst_ref=dst,
            send_sem=ssem,
            recv_sem=lat_rsem.at[rsem],
            device_id=(gg, ss),
            device_id_type=MESH,
        )

    main_at = jnp.where(low, s, 23 - s)

    def lat_sends(act):
        @pl.loop(0, 8)
        def _(j):
            k = (z + j + 4) % 8
            for a in range(2):

                @pl.when(jnp.logical_not(jnp.logical_and(j == 4, y == a)))
                def _():
                    act(
                        lat_copy(
                            lat_send.at[a],
                            lat_tok.at[main_at],
                            lat_ssem.at[a, k],
                            main_at,
                            g,
                            2 * k + a,
                        )
                    )

    lat_early = [
        lat_copy(
            lat_send.at[1 - a],
            lat_next.at[a],
            lat_ssem.at[2, a],
            16 + a,
            g if a == 0 else prev_g,
            15 - s,
        )
        for a in range(2)
    ]

    @pl.when(low)
    def _():
        for early in lat_early:
            early.start()
        lat_sends(lambda c: c.start())

    def o_copy(part, block, ssem, gg, ss):
        return pltpu.make_async_remote_copy(
            src_ref=o_buf.at[part, block_rows(block)],
            dst_ref=o_buf.at[part, block_rows(block)],
            send_sem=ssem,
            recv_sem=o_rsem.at[part, block],
            device_id=(gg, ss),
            device_id_type=MESH,
        )

    def seq_at(d):
        return 2 * ((z + d + 8) % 8) + y

    def column(d):
        return 8 * y + (z + d + 8) % 8

    def other(d):
        return 8 * (1 - y) + (z + d + 8) % 8

    def along(k, d):
        return o_copy(mine, me, z_ssem.at[k], g, seq_at(d))

    firsts = [along(k, d) for k, d in enumerate((2, -2, 1, -1))]
    side = 1 - 2 * core
    on_up = o_copy(mine, column(-2), z_ssem.at[4], g, seq_at(1))
    on_down = o_copy(mine, column(2), z_ssem.at[5], g, seq_at(-1))
    on_far = o_copy(mine, column(-2 * side), z_ssem.at[6], g, seq_at(2 * side))

    def across(block):
        return o_copy(mine, block, y_ssem.at[block % 8], y_g, y_s)

    def to_x(block):
        return o_copy(mine, block, x_ssem.at[block], x_g, s)

    def to_sib(part, block):
        return o_copy(part, block, sib_ssem.at[part // 2, block], sib_g, s)

    def arrived(part, block):
        o_copy(part, block, z_ssem.at[0], sib_g, s).wait_recv()

    def fold_copy(part, block, ssem, gg, ss):
        rows = pl.ds(pl.multiple_of(part * 48, 16), 48)
        return pltpu.make_async_remote_copy(
            src_ref=fold_buf.at[block, rows],
            dst_ref=fold_buf.at[block, rows],
            send_sem=ssem,
            recv_sem=fold_rsem.at[part, block],
            device_id=(gg, ss),
            device_id_type=MESH,
        )

    def fold_out(d):
        return fold_copy(core, me, fold_ssem.at[d], g, seq_at(d))

    def fold_across(block):
        return fold_copy(core, block, fy_ssem.at[block % 8], y_g, y_s)

    def fold_sib(block):
        return fold_copy(core, block, fsib_ssem.at[block], sib_g, s)

    def fold_arrived(part, block):
        fold_copy(part, block, fold_ssem.at[0], sib_g, s).wait_recv()

    fold_across(me).start()
    for d in (4, 3, 5, 2, 6, 1, 7):
        fold_out(d).start()

    for load in load_o:
        load.wait()
    for first in firsts:
        first.start()
    across(me).start()

    load_lens.wait()

    def length(node):
        last = lens_ref.shape[0] - 1
        return jnp.where(node <= last, lens_ref[jnp.minimum(node, last)], 0)

    @pl.when(jnp.logical_not(low))
    def _():
        row = lax.broadcasted_iota(jnp.int32, (PACK, 128), 0)
        col = lax.broadcasted_iota(jnp.int32, (PACK, 128), 1)
        at = 64 * (15 - s) + row + 32 * (col // 64)
        for a in range(2):
            lat_early[a].wait_recv()
            lat_send[a] = jnp.where(
                at < length(2 * g + a), lat_next[a].astype(F32), lat_send[a].astype(F32)
            ).astype(BF)
        lat_sends(lambda c: c.start())

    lat_tok[main_at] = lat_send[y]

    def variance(xt):
        gx = dot(gram_buf[...], xt.astype(BF))
        return jnp.maximum(jnp.sum((gx[:64] + gx[64:]) * xt, axis=0, keepdims=True), 0.0)

    tail_len = length(2 * g + y)

    def at_step(n):
        turn = n % 4
        near = (z // 2 + jnp.where(turn < 2, turn, 5 - turn)) % 4
        return 8 * jnp.where(n < 4, y, 1 - y) + 2 * near

    def fold_relay(n):
        for h in range(2):
            block = at_step(n) + h

            @pl.when(block != me)
            def _():
                fold_arrived(core, block)

                @pl.when(n < 4)
                def _():
                    fold_across(block).start()

                fold_sib(block).start()

    def around(d, of):
        return [
            (of(d), d >= 0),
            (of(-d), jnp.logical_and(d != 0, d != 4)),
        ]

    def pass_on_z(i):
        d = jnp.where(i == 0, 2, jnp.where(i == 1, 1, i + 1))
        for block, there in around(d, column):

            @pl.when(there)
            def _():
                arrived(mine, block)
                across(block).start()
                to_x(block).start()
                to_sib(mine, block).start()

        @pl.when(i == 0)
        def _():
            on_up.start()
            on_down.start()
            on_far.start()

    def pass_on_y(i):
        d = jnp.where(i == 1, 2, jnp.where(i == 2, 1, i))
        for block, there in around(d, other):

            @pl.when(there)
            def _():
                arrived(mine, block)
                to_x(block).start()
                to_sib(mine, block).start()

    theirs = 2 * (1 - px) + core

    def pass_on_x(d, of):
        for block, there in around(d, of):

            @pl.when(there)
            def _():
                arrived(theirs, block)
                to_sib(theirs, block).start()

    for n in range(4):
        fold_relay(jnp.int32(n))
    pass_on_z(jnp.int32(0))
    pass_on_z(jnp.int32(1))

    @pl.loop(0, 16)
    def _(k):
        @pl.when(k != main_at)
        def _():
            lat_copy(lat_send.at[0], lat_tok.at[k], lat_ssem.at[0, 0], k, sib_g, s).wait_recv()

    head_lines = lat_tok[0:8].astype(F32).reshape(256, 128)
    tail_lines = lat_tok[8:16].astype(F32).reshape(256, 128)
    tokens = jnp.concatenate([unpacked(head_lines), unpacked(tail_lines)], axis=0)
    xt = tokens.T
    xkt[0:64, :] = jnp.zeros((64, 1024), BF)
    xkt[64:128, :] = xt.astype(BF)
    var = variance(xt)
    key_eps = 1e-6 * (var + 1e-5)
    scaled = xt * lax.rsqrt(var + 1e-5)
    extra = (lax.broadcasted_iota(jnp.int32, (64, 1024), 0) == 0).astype(F32)
    w = jnp.concatenate([scaled, extra], axis=0).T
    w_head[...] = w[:512].astype(BF)
    place = lax.broadcasted_iota(jnp.int32, (512, 128), 0)
    tail_spot = 64 * ((place % 256) // 32) + place % 32 + 32 * (place // 256)
    w_tail[:, :128] = w[512:].astype(BF)
    w_tail[:, 128:] = jnp.where(tail_spot < tail_len, w[512:], 0.0).astype(BF)

    q_tail = lat_tok[8 + tail_block].astype(F32)
    q_tok = jnp.concatenate([unpacked(lat_tok[head_block].astype(F32)), unpacked(q_tail)], axis=0)
    q_xt = q_tok.T
    q_eps = 1e-6 * (variance(q_xt) + 1e-5)
    q_xtz = jnp.concatenate([q_xt.astype(BF), jnp.zeros((64, 128), BF)], axis=0)
    q_side = lax.broadcasted_iota(jnp.int32, (128, 128), 1) < 64

    def rms(x, eps, scale):
        parts = []
        for h in range(2):
            rows = x[64 * h : 64 * h + 64]
            mean = jnp.sum(rows * rows, axis=0, keepdims=True) * (1.0 / HDIM)
            parts.append(rows * (lax.rsqrt(mean + eps) * scale))
        return jnp.concatenate(parts, axis=0)


    def prepare(n):
        first = at_step(n)
        for h in range(2):

            @pl.when(first + h != me)
            def _():
                fold_arrived(1 - core, first + h)

    def keys_of(n, turn):
        pair = fold_buf[pl.ds(at_step(n), 2), 0:64]
        pair_qk = jnp.concatenate([pair[0], pair[1]], axis=0)
        key_buf[turn] = rms(dot(pair_qk, xkt[...]), key_eps, 1.0).astype(BF)
        query = rms(dot(pair_qk, q_xtz), q_eps, QSCALE).T
        query_buf[turn] = jnp.concatenate(
            [jnp.where(q_side, query, 0.0), jnp.where(q_side, 0.0, query)], axis=0
        ).astype(BF)

    prepare(jnp.int32(0))
    keys_of(jnp.int32(0), 0)

    @pl.loop(0, 8)
    def _(n):
        @pl.when(n < 4)
        def _():
            fold_relay(n + 4)

        later = jnp.minimum(n + 1, 7)

        @pl.when(n < 7)
        def _():
            prepare(later)

        first = at_step(n)
        pair = fold_buf[pl.ds(first, 2)]
        query2 = query_buf[n % 2]
        keys_t = key_buf[n % 2]
        keys_of(later, (n + 1) % 2)
        p = jnp.exp2(dot(query2, keys_t)).astype(BF)
        u_head = dot(p[:, :512], w_head[...])
        u_tail = dot(p[:, 512:], w_tail[...])
        u_all = u_head + u_tail[:, :128]
        ratio = u_all[:, :64] / u_all[:, 64:65]
        u_over = jnp.concatenate([u_tail[64:128, 128:], u_tail[192:256, 128:]], axis=0)
        total = u_over[:, 64:65]
        over = u_over[:, :64] / jnp.where(total == 0.0, 1.0, total)
        mean_even = jnp.concatenate([ratio[:128], over[:64]], axis=0).astype(BF)
        mean_odd = jnp.concatenate([ratio[128:], over[64:]], axis=0).astype(BF)
        att_even = dot(mean_even, unpacked(pair[0, 64:96].astype(F32)).astype(BF))
        att_odd = dot(mean_odd, unpacked(pair[1, 64:96].astype(F32)).astype(BF))
        columns = pl.ds(pl.multiple_of(first * 64, 128), 128)
        att[:, columns] = jnp.concatenate([att_even, att_odd], axis=1).astype(BF)

        @pl.when(jnp.logical_and(n >= 1, n < 3))
        def _():
            pass_on_z(n + 1)

        @pl.when(jnp.logical_and(n >= 1, n < 6))
        def _():
            pass_on_y(n - 1)

        @pl.when(jnp.logical_and(n >= 3, n < 7))
        def _():
            i = n - 3
            pass_on_x(jnp.where(i == 0, 2, jnp.where(i == 1, 1, i + 1)), column)


    tok2 = jnp.concatenate([q_tok, q_tok[64:]], axis=0).astype(BF)
    def project(part):
        columns = pl.ds(pl.multiple_of(part * quarter, 128), quarter)
        mix[:, columns] = dot(att[...], o_buf[part]) + dot(tok2, wi_ref[:, columns])

    def from_sib(part):
        @pl.loop(1, 16)
        def _(k):
            arrived(part, (me + k) % 16)

    for d in (0, 2, 1, 3, 4):
        pass_on_x(jnp.int32(d), other)
    project(mine)
    from_sib(2 * px + 1 - core)
    project(2 * px + 1 - core)
    project(theirs)
    from_sib(2 * (1 - px) + 1 - core)
    project(2 * (1 - px) + 1 - core)
    mixed = mix[...]
    mean = jnp.mean(mixed, axis=1, keepdims=True)
    centre = mixed - mean
    spread = jnp.mean(centre * centre, axis=1, keepdims=True)
    load_fgain.wait()
    load_ho.wait()
    final = (centre * lax.rsqrt(spread + 1e-5) * fgain_ref[...].reshape(1, -1)).astype(BF)
    score = dot_nt(final, ho_v[...])

    where_t = 64 * tail_block + lax.broadcasted_iota(jnp.int32, (64, 64), 0)
    counted = where_t < tail_len
    sc_send[0] = packed(score[:64])
    sc_send[1] = packed(jnp.where(counted, score[64:128] - score[128:], 0.0))
    tail_g = jnp.where(y == 0, g, next_g)
    targets = [(g, head_block, y), (tail_g, tail_block, 3 - y), (g, 15 - tail_block, y)]

    def sc_copy(k, gg, ss, at):
        return pltpu.make_async_remote_copy(
            src_ref=sc_send.at[k],
            dst_ref=sc_recv.at[at],
            send_sem=sc_ssem.at[k],
            recv_sem=sc_rsem.at[at],
            device_id=(gg, ss),
            device_id_type=MESH,
        )

    own = [s == head_block, jnp.logical_and(y == 0, s == tail_block), s == 15 - tail_block]

    for k, (gg, ss, at) in enumerate(targets):
        if k == 2:
            turned = jnp.dot(
                reversal(),
                jnp.where(counted, 0.0, score[64:128]),
                precision=lax.Precision.HIGHEST,
                preferred_element_type=F32,
            )
            sc_send[2] = packed(turned)


        @pl.when(jnp.logical_not(own[k]))
        def _():
            sc_copy(k, gg, ss, at).start()

        @pl.when(own[k])
        def _():
            sc_recv[at] = sc_send[k]

    lat_sends(lambda c: c.wait_send())

    @pl.when(low)
    def _():
        for early in lat_early:
            early.wait_send()

    @pl.loop(1, 16)
    def _(k):
        there = (me + k) % 16
        fold_sib(there).wait_send()
        to_x(there).wait_send()
        to_sib(mine, there).wait_send()
        to_sib(theirs, there).wait_send()

    @pl.loop(1, 8)
    def _(d):
        fold_out(d).wait_send()

    for sent in (*firsts, on_up, on_down, on_far):
        sent.wait_send()

    @pl.loop(0, 8)
    def _(k):
        across(8 * y + k).wait_send()
        fold_across(8 * y + k).wait_send()

    @pl.when(jnp.logical_not(low))
    def _():
        sc_recv[2] = jnp.zeros((PACK, 128), F32)
        sc_recv[3] = jnp.zeros((PACK, 128), F32)

    kept = jnp.logical_or(own[0], own[2])
    for a in range(2):

        @pl.when(jnp.logical_not(jnp.logical_and(kept, y == a)))
        def _():
            sc_copy(0, g, s, a).wait_recv()

    @pl.when(low)
    def _():
        sc_copy(0, g, s, 2).wait_recv()

        @pl.when(jnp.logical_not(own[1]))
        def _():
            sc_copy(0, g, s, 3).wait_recv()

    row = 64 * s + lax.broadcasted_iota(jnp.int32, (64, 64), 0)
    for a in range(2):
        slot = 2 * g + a
        gone = length(slot)
        step = lat_ref[a] + STEP * unpacked(sc_recv[a] + sc_recv[2 + a])
        out_ref[a] = jnp.where(row < 1024 - gone, step, 0.0)

    for k in range(3):

        @pl.when(jnp.logical_not(own[k]))
        def _():
            sc_copy(k, g, s, 0).wait_send()


def solution(mesh):
    groups = mesh.shape["group"]

    def body(latent, margin_len, in_weight, norm_gain, qkv_weight, out_weight, final_gain, head_out):
        width = in_weight.shape[1]
        vmem = pl.BlockSpec(memory_space=pltpu.VMEM)
        hbm = pl.BlockSpec(memory_space=pl.ANY)
        dma = pltpu.SemaphoreType.DMA
        return pl.pallas_call(
            functools.partial(kernel, groups),
            out_shape=jax.ShapeDtypeStruct(latent.shape, F32),
            in_specs=[hbm] * 8,
            out_specs=vmem,
            scratch_shapes=[
                pltpu.VMEM(latent.shape, F32),
                pltpu.SMEM(margin_len.shape, jnp.int32),
                pltpu.VMEM(in_weight.shape, BF),
                pltpu.VMEM((width,), F32),
                pltpu.VMEM((3, HDIM, width), BF),
                pltpu.VMEM((width,), F32),
                pltpu.VMEM(head_out.shape[::-1], BF),
                pltpu.VMEM((2, PACK, 128), BF),
                pltpu.VMEM((16, PACK, 128), BF),
                pltpu.VMEM((2, PACK, 128), BF),
                pltpu.VMEM((16, 96, 128), BF),
                pltpu.VMEM((128, HDIM), BF),
                pltpu.VMEM((4, 1024, width // 4), BF),
                pltpu.VMEM((128, 1024), BF),
                pltpu.VMEM((512, 128), BF),
                pltpu.VMEM((512, 256), BF),
                pltpu.VMEM((192, 1024), BF),
                pltpu.VMEM((192, width), F32),
                pltpu.VMEM((2, 128, 1024), BF),
                pltpu.VMEM((2, 256, 128), BF),
                pltpu.VMEM((3, PACK, 128), F32),
                pltpu.VMEM((4, PACK, 128), F32),
                dma((7,)),
                dma((4,)),
                dma((3, 8)),
                dma((24,)),
                dma((8,)),
                dma((8,)),
                dma((16,)),
                dma((2, 16)),
                dma((8,)),
                dma((8,)),
                dma((16,)),
                dma((2, 16)),
                dma((4, 16)),
                dma((3,)),
                dma((4,)),
            ],
            compiler_params=pltpu.CompilerParams(
                collective_id=0, has_side_effects=True, vmem_limit_bytes=60 * 1024 * 1024
            ),
        )(
            latent,
            margin_len,
            in_weight,
            norm_gain,
            jnp.swapaxes(qkv_weight, 1, 2),
            out_weight,
            final_gain,
            head_out.T,
        )

    in_specs = (
        P("group", "seq", None),
        P(),
        P(),
        P(),
        P(None, None, "seq"),
        P("seq", None),
        P(),
        P(),
    )
    return jax.shard_map(
        body, mesh=mesh, in_specs=in_specs, out_specs=P("group", "seq", None), check_vma=False
    )
```
